128 devices in a mesh: ctx: 16 (over z, y), exp: 8 (over x, core).
Axes of the slice: x: 4, y: 4, z: 4, core: 2. Of those that a mesh axis runs over, the one named last changes fastest.
Arguments:
- attention: bfloat16 [8, 2048, 4096], P('exp', None, 'ctx'), may hold values from -6 to 6
- out_weight: bfloat16 [4096, 2880], P('ctx', 'exp'), may hold values from -0.09375 to 0.09375
- norm_gain: float32 [2880], replicated, may hold values from 0.1 to 1.9
- w_gate: bfloat16 [128, 2880, 1440], P(('ctx', 'exp')), may hold values from -0.109375 to 0.109375
- w_up: bfloat16 [128, 2880, 1440], P(('ctx', 'exp')), may hold values from -0.109375 to 0.109375
- w_down: bfloat16 [128, 1440, 2880], P(('ctx', 'exp')), may hold values from -0.15625 to 0.15625
- routes: int32 [8, 2048, 4], P('exp', 'ctx'), may hold values from 0 to 127, all different within a row; in each aligned block of 128 rows (0 to 127, 128 to 255, ..., all dimensions but the last counted through in order) at most 6 rows name the same one
- gate_fixed: int32 [8, 2048, 4], P('exp', 'ctx'), may hold values from 1 to 65536
Outputs:
- layer_out: bfloat16 [8, 2048, 2880], P('exp', 'ctx')
The draws below stay inside these ranges and needn't reach their ends.
Inputs may be any that keep to these rules, and one draw needn't show every extreme that they name: `routes`: each token names four different experts. Among the 128 tokens of one device no expert is named by more than 6 tokens, a bound that some block reaches.
All inputs are finite; a program needn't handle non-finite values.
Results may differ from the reference program's by a relative error of at most 0.02.
Values may be sent and summed in bfloat16 or wider, within the bound.
A program may use at most 128 MiB of HBM per device.

```python
import math
import jax
import jax.numpy as jnp
import numpy as np
from jax import lax

D = 2880
FFW = 1440
TOK_DEV = 128
HD = 4096
SEQS = 8
LEN = 2048
EXPERTS = 128
CAP = 6


def set_ends(drawn, rng, smallest, high):
    place = [jax.random.randint(jax.random.fold_in(rng, axis), (), 0, length) for axis, length in enumerate(drawn.shape)]
    main_axis = drawn.shape.index(max(drawn.shape))
    next_to = place[:main_axis] + [(place[main_axis] + 1) % drawn.shape[main_axis]] + place[main_axis + 1:]
    return drawn.at[tuple(place)].set(smallest).at[tuple(next_to)].set(high)


def levels(rng, dims, pieces, smallest, largest):
    loudness, own = 1.0, jax.random.fold_in(rng, 6)
    for dim, parts in pieces:
        draws = jnp.exp(jax.random.uniform(jax.random.fold_in(own, dim), (parts,), jnp.float32, smallest / len(pieces), largest / len(pieces)))
        loudness = loudness * jnp.repeat(draws, dims[dim] // parts).reshape([-1 if axis == dim else 1 for axis in range(len(dims))])
    return loudness


def assign_block(key, own, number, rows, amount, top, reach, lean):
    order = jax.random.permutation(key, amount)
    crowded, ordinary = load_shares(amount, rows * top, reach, lean, True), load_shares(amount, rows * top, reach, lean, False)
    places = jnp.arange(amount)

    def named(sizes, rotation):
        used = int((sizes > 0).sum())
        fixed = max(1, used // 4)
        moved = fixed + (places - fixed + rotation * (used - fixed)) % max(1, amount - fixed)
        return jnp.zeros((amount,), jnp.int32).at[order[jnp.where(places < fixed, places, moved)]].set(jnp.asarray(sizes, jnp.int32))

    sizes = jnp.where(number % 4 == 0, named(crowded, number // 4), named(ordinary, number - number // 4 - 1))
    mixed = jax.random.permutation(jax.random.fold_in(own, 3), amount)
    source_of, sink = mixed[0:amount // 2 * 2:2], mixed[1:amount // 2 * 2:2]
    room = jnp.minimum(sizes[source_of] - 1, reach - sizes[sink]) // 2
    room = jnp.where((source_of == order[0]) | (sink == order[0]) | (sizes[sink] == 0), 0, jnp.maximum(room, 0))
    moved = jax.random.randint(jax.random.fold_in(own, 4), (amount // 2,), 0, 1 << 20) % (room + 1)
    sizes = sizes.at[source_of].add(-moved).at[sink].add(moved)
    labels = jnp.searchsorted(jnp.cumsum(sizes), jnp.arange(rows * top), side="right").astype(jnp.int32)
    grid = labels.reshape(top, rows).T
    grid = grid[jax.random.permutation(jax.random.fold_in(own, 1), rows)]
    rotation = jax.random.randint(jax.random.fold_in(own, 2), (rows, 1), 0, top)
    return jnp.take_along_axis(grid, (jnp.arange(top)[None, :] + rotation) % top, axis=1)


def load_shares(count, total, limit, slope, full):
    weights = [(1 << 20) // math.isqrt(standing ** slope) + 1 for standing in range(1, count + 1)]
    largest = limit if full else min(limit, max(-(-total // count), total * weights[0] // sum(weights)))
    least = 1 if total - largest >= count - 1 else 0
    holding, rest = [largest] + [least] * (count - 1), total - largest - least * (count - 1)
    while rest > 0:
        free = [i for i in range(1, count) if holding[i] < largest] or [i for i in range(1, count) if holding[i] < limit]
        whole, remaining = sum([weights[i] for i in free]), rest
        for i in free:
            extra = min(limit - holding[i], max(1, remaining * weights[i] // whole), rest)
            holding[i] = holding[i] + extra
            rest = rest - extra
    return np.array(holding)


def gaussian(key, dims, width, limit, shards=(), kind=jnp.bfloat16):
    level = levels(key, dims, shards, -0.22, 0.18) if shards else 1.0
    drawn = jax.random.normal(key, dims, jnp.float32) * width * level
    return jnp.minimum(jnp.maximum(drawn, -limit), limit).astype(kind)


def setup_inputs(seed: int = 0) -> dict:
    splits = jax.random.split(jax.random.key(seed), 9)
    attention = gaussian(splits[0], (SEQS, LEN, HD), 1.0, 6.0, ((0, 8), (2, 16)))
    out_weight = gaussian(splits[1], (HD, D), HD ** -0.5, 0.09375, ((0, 16), (1, 8)))
    norm_gain = jnp.clip(1.0 + 0.18 * jax.random.normal(splits[2], (D,), jnp.float32), 0.1, 1.9)
    w_gate = gaussian(splits[3], (EXPERTS, D, FFW), D ** -0.5, 0.109375, ((0, 128),))
    w_up = gaussian(splits[4], (EXPERTS, D, FFW), D ** -0.5, 0.109375, ((0, 128),))
    w_down = gaussian(splits[5], (EXPERTS, FFW, D), FFW ** -0.5, 0.15625, ((0, 128),))
    routes_keys = jax.random.split(jax.random.fold_in(splits[6], 1), SEQS * LEN // TOK_DEV)
    routes_turns = jax.random.permutation(jax.random.fold_in(splits[6], 3), SEQS * LEN // TOK_DEV)
    routes = jax.vmap(lambda own, number: assign_block(jax.random.fold_in(splits[6], 2), own, number, TOK_DEV, EXPERTS, 4, CAP, 2))(routes_keys, routes_turns).reshape((SEQS, LEN, 4))
    gate_fixed = set_ends(jax.random.randint(splits[7], (SEQS, LEN, 4), 1, 65537), jax.random.fold_in(splits[7], 1), 1, 65536).astype(jnp.int32)
    return {"attention": attention, "out_weight": out_weight, "norm_gain": norm_gain, "w_gate": w_gate, "w_up": w_up, "w_down": w_down, "routes": routes, "gate_fixed": gate_fixed}


def reference(attention, out_weight, norm_gain, w_gate, w_up, w_down, routes, gate_fixed):
    flat_heads = attention.reshape(-1, attention.shape[-1])
    projected = jnp.dot(flat_heads, out_weight, preferred_element_type=jnp.float32).astype(jnp.bfloat16)
    widened = projected.astype(jnp.float32)
    scale_rows = lax.rsqrt(lax.optimization_barrier(jnp.mean(widened * widened, axis=-1, keepdims=True)) + 1e-05)
    normed = (widened * scale_rows * norm_gain.astype(jnp.float32)).astype(jnp.bfloat16)
    expert_ids = routes.reshape(-1).astype(jnp.int32)
    pair_count = expert_ids.shape[0]
    token_index = (jnp.arange(pair_count, dtype=jnp.int32) // 4).astype(jnp.int32)
    weights = gate_fixed.reshape(-1).astype(jnp.float32) / 65536.0
    order = jnp.argsort(expert_ids, stable=True).astype(jnp.int32)
    counts = lax.optimization_barrier(jnp.sum((expert_ids[None, :] == jnp.arange(EXPERTS, dtype=jnp.int32)[:, None]).astype(jnp.int32), axis=1))
    offsets = (jnp.cumsum(counts) - counts).astype(jnp.int32)
    most_rows = EXPERTS * CAP
    padded_order = jnp.concatenate([order, jnp.zeros((most_rows,), jnp.int32)])

    def one_expert(running, expert):
        picked = lax.dynamic_slice_in_dim(padded_order, offsets[expert].astype(jnp.int32), most_rows)
        valid = (jnp.arange(most_rows, dtype=jnp.int32) < counts[expert]).astype(jnp.float32)
        targets = token_index[picked]
        arrived = normed[targets]
        gate_value = jnp.dot(arrived, w_gate[expert], preferred_element_type=jnp.float32)
        up_value = jnp.dot(arrived, w_up[expert], preferred_element_type=jnp.float32)
        activated = (gate_value * jax.nn.sigmoid(1.702 * gate_value) * (up_value + 1.0)).astype(jnp.bfloat16)
        result = jnp.dot(activated, w_down[expert], preferred_element_type=jnp.float32).astype(jnp.bfloat16)
        scaled = result.astype(jnp.float32) * (weights[picked] * valid)[:, None]
        return (running.at[targets].add(scaled), None)
    combined, unused = lax.scan(one_expert, jnp.zeros(widened.shape, jnp.float32), jnp.arange(EXPERTS, dtype=jnp.int32))
    layer_out = (widened + combined).astype(jnp.bfloat16)
    return layer_out.reshape(attention.shape[0], attention.shape[1], widened.shape[1])
```

```python
import functools

import jax
import jax.numpy as jnp
from jax import lax
from jax.experimental import pallas as pl
from jax.experimental.pallas import tpu as pltpu
from jax.sharding import PartitionSpec as P

MESH = pl.DeviceIdType.MESH
BF16, F32, I32 = jnp.bfloat16, jnp.float32, jnp.int32

D = 2880
FFW = 1440
TOK = 128
CAP = 6
DEV = 128
SLICE = 384
PIECES = 8
WIDE = SLICE * PIECES
ROWS = PIECES * CAP
BLOCK = 8
BROWS = BLOCK * CAP
GROUP = 32
GROUPS = DEV // GROUP
GROWS = GROUP * CAP
VMEM = 56 * 1024 * 1024


def offsets(slot):
    group, rest = slot // GROUP, slot % GROUP
    dz, dy, dc = rest // 8, (rest // 2) % 4, rest % 2
    return dz, dy, (group + 8 - dz - dy) % 4, dc


def partner(slot, back):
    ctx, exp = lax.axis_index("ctx"), lax.axis_index("exp")
    dz, dy, dx, dc = offsets(slot)
    if back:
        dz, dy, dx = 4 - dz, 4 - dy, 4 - dx
    z, y = (ctx // 4 + dz) % 4, (ctx % 4 + dy) % 4
    x, core = (exp // 2 + dx) % 4, (exp % 2 + dc) % 2
    return z * 4 + y, x * 2 + core


def unpack(mixer, messages):
    flat = messages.reshape(BLOCK * ROWS, SLICE)
    sorted_rows = jnp.dot(mixer, flat, preferred_element_type=F32).astype(BF16)
    return [sorted_rows[piece * BROWS : (piece + 1) * BROWS] for piece in range(PIECES)]


def pack(mixer_t, rows):
    stacked = jnp.concatenate(
        [rows[:, piece * SLICE : (piece + 1) * SLICE] for piece in range(PIECES)], axis=0
    )
    mixed = jnp.dot(mixer_t, stacked, preferred_element_type=F32).astype(BF16)
    return mixed.reshape(BLOCK, ROWS, SLICE)


def mixers():
    count = BLOCK * ROWS
    place = jnp.arange(count, dtype=I32)
    piece, position, message = place // BROWS, (place // BLOCK) % CAP, place % BLOCK
    source = message * ROWS + piece * CAP + position
    mixer = (source[:, None] == place[None, :]).astype(BF16)
    mixer_t = (place[:, None] == source[None, :]).astype(BF16)
    return mixer, mixer_t


def slot_columns():
    column = jnp.arange(DEV * CAP, dtype=I32)
    block, position, message = column // BROWS, (column // BLOCK) % CAP, column % BLOCK
    ctx, exp = partner(block * BLOCK + message, False)
    return (ctx * 8 + exp).reshape(1, -1).astype(I32), position.reshape(1, -1)


def slot_mask(routes, expert_col, position_col):
    named = [(routes[:, k : k + 1] == expert_col) for k in range(4)]
    chosen = named[0] | named[1] | named[2] | named[3]
    earlier = lax.broadcasted_iota(I32, (TOK, TOK), 1) < lax.broadcasted_iota(I32, (TOK, TOK), 0)
    rank = jnp.dot(
        jnp.where(earlier, 1.0, 0.0).astype(BF16),
        jnp.where(chosen, 1.0, 0.0).astype(BF16),
        preferred_element_type=F32,
    )
    return named, chosen & (rank == position_col.astype(F32))


def dispatch_kernel(projected, gain, routes, expert_col, position_col, mixer_t, send, normed, rows):
    widened = projected[...].astype(F32)
    scale = lax.rsqrt(jnp.mean(widened * widened, axis=-1, keepdims=True) + 1e-05)
    normed[:, D:] = jnp.zeros((TOK, WIDE - D), BF16)
    normed[:, :D] = (widened * scale * gain[...]).astype(BF16)
    _, mask = slot_mask(routes[...], expert_col[...], position_col[...])
    chooser = jnp.transpose(jnp.where(mask, 1.0, 0.0)).astype(BF16)

    @pl.loop(0, PIECES)
    def _(piece):
        columns = pl.ds(pl.multiple_of(piece * SLICE, SLICE), SLICE)
        rows[:, columns] = jnp.dot(
            chooser, normed[:, columns], preferred_element_type=F32
        ).astype(BF16)

    @pl.loop(0, DEV // BLOCK)
    def _(block):
        here = pl.ds(pl.multiple_of(block * BROWS, BROWS), BROWS)
        send[pl.ds(block * BLOCK, BLOCK)] = pack(mixer_t[...], rows[here, :])


def combine_kernel(
    returned, projected, routes, gate_fixed, expert_col, position_col, mixer, out, rows
):
    @pl.loop(0, DEV // BLOCK)
    def _(block):
        here = pl.ds(pl.multiple_of(block * BROWS, BROWS), BROWS)
        pieces = unpack(mixer[...], returned[pl.ds(block * BLOCK, BLOCK)])
        for piece in range(PIECES):
            rows[here, piece * SLICE : (piece + 1) * SLICE] = pieces[piece]

    named, mask = slot_mask(routes[...], expert_col[...], position_col[...])
    fixed = jnp.zeros((TOK, DEV * CAP), I32)
    for k in range(4):
        fixed = fixed + jnp.where(named[k], gate_fixed[:, k : k + 1], 0)
    fixed = jnp.where(mask, fixed, 0)
    high = (fixed // 256).astype(F32).astype(BF16)
    low = (fixed % 256).astype(F32).astype(BF16)
    weights = jnp.concatenate([high, low], axis=0)
    for start in range(0, D, SLICE):
        stop = min(start + SLICE, D)
        total = jnp.dot(weights, rows[:, start:stop], preferred_element_type=F32)
        combined = total[:TOK] * (1.0 / 256.0) + total[TOK:] * (1.0 / 65536.0)
        out[:, start:stop] = (projected[:, start:stop].astype(F32) + combined).astype(BF16)


def expert_kernel(
    send, w_gate, w_up, w_down, mixer, mixer_t,
    returned,
    gate, up, down, landed, results, arrived, activated, outputs,
    weight_sems, send_sem, land_sems, result_sem, return_sem,
):
    loads = [
        pltpu.make_async_copy(source.at[0], target, weight_sems.at[i])
        for i, (source, target) in enumerate(((w_gate, gate), (w_up, up), (w_down, down)))
    ]
    for load in loads:
        load.start()
    barrier = pltpu.get_barrier_semaphore()

    @pl.loop(1, DEV)
    def _(slot):
        pl.semaphore_signal(barrier, inc=1, device_id=partner(slot, False), device_id_type=MESH)

    pl.semaphore_wait(barrier, DEV - 1)
    own = pltpu.make_async_copy(send.at[0], landed.at[0], land_sems.at[0])
    own.start()

    @pl.loop(1, DEV)
    def _(slot):
        pltpu.make_async_remote_copy(
            src_ref=send.at[slot],
            dst_ref=landed.at[slot],
            send_sem=send_sem,
            recv_sem=land_sems.at[slot // GROUP],
            device_id=partner(slot, False),
            device_id_type=MESH,
        ).start()

    outputs[:, D:] = jnp.zeros((GROWS, WIDE - D), BF16)
    for load in loads:
        load.wait()

    @pl.loop(0, GROUPS)
    def _(group):
        first = group * GROUP
        span = landed.at[pl.ds(first, GROUP)]
        pltpu.make_async_copy(span, span, land_sems.at[group]).wait()

        @pl.loop(0, GROUP // BLOCK)
        def _(block):
            here = pl.ds(pl.multiple_of(block * BROWS, BROWS), BROWS)
            pieces = unpack(mixer[...], landed[pl.ds(first + block * BLOCK, BLOCK)])
            for piece in range(PIECES):
                arrived[here, piece * SLICE : (piece + 1) * SLICE] = pieces[piece]

        def hidden(columns):
            gate_value = jnp.dot(arrived[:, :D], gate[:, columns], preferred_element_type=F32)
            up_value = jnp.dot(arrived[:, :D], up[:, columns], preferred_element_type=F32)
            activated[:, columns] = (
                gate_value / (1.0 + jnp.exp(-1.702 * gate_value)) * (up_value + 1.0)
            ).astype(BF16)

        @pl.loop(0, FFW // 256)
        def _(tile):
            hidden(pl.ds(pl.multiple_of(tile * 256, 256), 256))

        hidden(pl.ds(FFW // 256 * 256, FFW % 256))

        def projected_down(columns):
            outputs[:, columns] = jnp.dot(
                activated[...], down[:, columns], preferred_element_type=F32
            ).astype(BF16)

        @pl.loop(0, D // 256)
        def _(tile):
            projected_down(pl.ds(pl.multiple_of(tile * 256, 256), 256))

        projected_down(pl.ds(D // 256 * 256, D % 256))

        @pl.loop(0, GROUP // BLOCK)
        def _(block):
            here = pl.ds(pl.multiple_of(block * BROWS, BROWS), BROWS)
            results[pl.ds(first + block * BLOCK, BLOCK)] = pack(mixer_t[...], outputs[here, :])

        @pl.when(group == 0)
        def _():
            pltpu.make_async_copy(results.at[0], returned.at[0], return_sem).start()

        @pl.loop(jnp.maximum(first, 1), first + GROUP)
        def _(slot):
            pltpu.make_async_remote_copy(
                src_ref=results.at[slot],
                dst_ref=returned.at[slot],
                send_sem=result_sem,
                recv_sem=return_sem,
                device_id=partner(slot, True),
                device_id_type=MESH,
            ).start()

    sent = send.at[pl.ds(1, DEV - 1)]
    pltpu.make_async_copy(sent, sent, send_sem).wait()
    sent = results.at[pl.ds(1, DEV - 1)]
    pltpu.make_async_copy(sent, sent, result_sem).wait()
    pltpu.make_async_copy(returned, returned, return_sem).wait()


def whole(count):
    return [pl.BlockSpec(memory_space=pltpu.VMEM)] * count


def project(attention, out_weight):
    along_z = [[y, 4 + y, 8 + y, 12 + y] for y in range(4)]
    along_y = [[4 * z, 4 * z + 1, 4 * z + 2, 4 * z + 3] for z in range(4)]
    tokens = lax.all_to_all(
        attention[0], "ctx", split_axis=0, concat_axis=1, tiled=True, axis_index_groups=along_z
    )
    weight = lax.all_gather(out_weight, "exp", axis=1, tiled=True)
    weight = lax.all_gather(weight, "ctx", axis=0, tiled=True, axis_index_groups=along_z)
    partial = jnp.dot(tokens, weight, preferred_element_type=F32).astype(BF16)
    parts = lax.all_to_all(
        partial.reshape(4, TOK, D), "ctx", split_axis=0, concat_axis=0, tiled=True,
        axis_index_groups=along_y,
    )
    return jnp.sum(parts.astype(F32), axis=0).astype(BF16)


def shards(attention, out_weight, norm_gain, w_gate, w_up, w_down, routes, gate_fixed):
    mixer, mixer_t = mixers()
    expert_col, position_col = slot_columns()
    projected = project(attention, out_weight)
    message = jax.ShapeDtypeStruct((DEV, ROWS, SLICE), BF16)
    params = pltpu.CompilerParams(vmem_limit_bytes=VMEM)
    send = pl.pallas_call(
        dispatch_kernel,
        out_shape=message,
        in_specs=whole(6),
        out_specs=whole(1)[0],
        scratch_shapes=[pltpu.VMEM((TOK, WIDE), BF16), pltpu.VMEM((DEV * CAP, WIDE), BF16)],
        compiler_params=params,
    )(projected, norm_gain.reshape(1, D), routes[0], expert_col, position_col, mixer_t)
    anywhere = pl.BlockSpec(memory_space=pl.ANY)
    returned = pl.pallas_call(
        expert_kernel,
        out_shape=message,
        in_specs=[anywhere] * 4 + whole(2),
        out_specs=anywhere,
        scratch_shapes=[
            pltpu.VMEM((D, FFW), BF16),
            pltpu.VMEM((D, FFW), BF16),
            pltpu.VMEM((FFW, D), BF16),
            pltpu.VMEM((DEV, ROWS, SLICE), BF16),
            pltpu.VMEM((DEV, ROWS, SLICE), BF16),
            pltpu.VMEM((GROWS, WIDE), BF16),
            pltpu.VMEM((GROWS, FFW), BF16),
            pltpu.VMEM((GROWS, WIDE), BF16),
            pltpu.SemaphoreType.DMA((3,)),
            pltpu.SemaphoreType.DMA,
            pltpu.SemaphoreType.DMA((GROUPS,)),
            pltpu.SemaphoreType.DMA,
            pltpu.SemaphoreType.DMA,
        ],
        compiler_params=pltpu.CompilerParams(
            vmem_limit_bytes=VMEM, collective_id=0, has_side_effects=True
        ),
    )(send, w_gate, w_up, w_down, mixer, mixer_t)
    out = pl.pallas_call(
        combine_kernel,
        out_shape=jax.ShapeDtypeStruct((TOK, D), BF16),
        in_specs=whole(7),
        out_specs=whole(1)[0],
        scratch_shapes=[pltpu.VMEM((DEV * CAP, WIDE), BF16)],
        compiler_params=params,
    )(returned, projected, routes[0], gate_fixed[0], expert_col, position_col, mixer)
    return out[None]


def solution(mesh):
    in_specs = (
        P("exp", None, "ctx"),
        P("ctx", "exp"),
        P(),
        P(("ctx", "exp"), None, None),
        P(("ctx", "exp"), None, None),
        P(("ctx", "exp"), None, None),
        P("exp", "ctx", None),
        P("exp", "ctx", None),
    )
    out_specs = P("exp", "ctx", None)
    return jax.shard_map(shards, mesh=mesh, in_specs=in_specs, out_specs=out_specs, check_vma=False)
```

```python
import jax
import jax.numpy as jnp
from jax import lax
from jax.experimental import pallas as pl
from jax.experimental.pallas import tpu as pltpu
from jax.sharding import PartitionSpec as P

MESH = pl.DeviceIdType.MESH
BF16, F32, I32 = jnp.bfloat16, jnp.float32, jnp.int32
NT = (((1,), (1,)), ((), ()))

D = 2880
FFW = 1440
TOK = 128
HEAD = 256
COLS = 360
SPAN = 4 * TOK
CAP = 6
DEV = 128
SLICE = 384
PIECES = 8
WIDE = SLICE * PIECES
ROWS = PIECES * CAP
BLOCK = 8
BROWS = BLOCK * CAP
GROUP = 32
GROUPS = DEV // GROUP
GROWS = GROUP * CAP
VMEM = 60 * 1024 * 1024


def ahead():
    ctx, exp = lax.axis_index("ctx"), lax.axis_index("exp")
    z, y = lax.div(ctx, 4), lax.rem(ctx, 4)
    x, core = lax.div(exp, 2), lax.rem(exp, 2)
    zs = [lax.rem(z + step, 4) for step in range(4)]
    ys = [lax.rem(y + step, 4) for step in range(4)]
    xs = [lax.rem(x + step, 4) for step in range(4)]
    cores = [core, 1 - core]
    return zs, ys, xs, cores


def project_kernel(
    attention, weight, out, heads, wide, partial, landed,
    own_sems, head_sems, wide_sems, half_sems, part_sems, relay_sems, send_sems,
):
    zs, ys, xs, cores = ahead()

    def device(dz=0, dy=0, dx=0, dc=0):
        return zs[dz] * 4 + ys[dy], xs[dx] * 2 + cores[dc]

    def lanes(dz, start=0, count=HEAD):
        return pl.ds(dz * HEAD + start, count)

    def remote(source, target, send, receive, **offset):
        pltpu.make_async_remote_copy(
            src_ref=source, dst_ref=target, send_sem=send_sems.at[send], recv_sem=receive,
            device_id=device(**offset), device_id_type=MESH,
        ).start()

    def arrival(target, semaphore):
        pltpu.make_async_copy(target, target, semaphore).wait()

    own_heads = attention.at[pl.ds(pl.multiple_of(zs[0] * SPAN, SPAN), SPAN)]
    own = [
        pltpu.make_async_copy(weight, wide.at[0, :, lanes(0)], own_sems.at[0]),
        pltpu.make_async_copy(own_heads, heads.at[:, lanes(0)], own_sems.at[1]),
    ]
    for copy in own:
        copy.start()
    barrier = pltpu.get_barrier_semaphore()
    friends = (
        [dict(dz=d) for d in (1, 2, 3)] + [dict(dy=d) for d in (1, 2, 3)]
        + [dict(dx=1), dict(dx=3), dict(dc=1)]
    )
    for offset in friends:
        pl.semaphore_signal(barrier, inc=1, device_id=device(**offset), device_id_type=MESH)
    pl.semaphore_wait(barrier, len(friends))

    for dz in (1, 3, 2):
        remote(weight, wide.at[0, :, lanes(dz)], 0, wide_sems.at[dz, 0], dz=dz)
    for dz in (1, 3, 2):
        block = attention.at[pl.ds(pl.multiple_of(zs[dz] * SPAN, SPAN), SPAN)]
        remote(block, heads.at[:, lanes(dz)], 1, head_sems.at[dz], dz=dz)

    def across(dz, dx):
        slot = wide.at[2 * dx, :, lanes(dz)]
        remote(slot, wide.at[2 * dx + 1, :, lanes(dz)], 2, wide_sems.at[dz, 2 * dx + 1], dc=1)

    def sideways(dz):
        slot = wide.at[0, :, lanes(dz)]
        if dz:
            arrival(slot, wide_sems.at[dz, 0])
        else:
            own[0].wait()
        for dx in (1, 3):
            remote(slot, wide.at[2 * dx, :, lanes(dz)], 3, wide_sems.at[dz, 2 * dx], dx=dx)
        across(dz, 0)

    def relay(dz):
        for dx, start, semaphore in ((1, 0, wide_sems.at[dz, 4]), (3, 128, half_sems.at[dz])):
            arrival(wide.at[2 * dx, :, lanes(dz)], wide_sems.at[dz, 2 * dx])
            remote(
                wide.at[2 * dx, :, lanes(dz, start, 128)], wide.at[4, :, lanes(dz, start, 128)],
                4, semaphore, dx=dx,
            )
            across(dz, dx)

    def far(dz):
        arrival(wide.at[4, :, lanes(dz, 0, 128)], wide_sems.at[dz, 4])
        arrival(wide.at[4, :, lanes(dz, 128, 128)], half_sems.at[dz])
        across(dz, 2)

    def column(group):
        return xs[(4 - group // 2) % 4] * 2 + cores[group % 2]

    pending = []

    def multiply(group):
        if group % 2:
            for dz in range(4):
                arrival(wide.at[group, :, lanes(dz)], wide_sems.at[dz, group])
        product = lax.dot_general(
            wide[group], heads[...], NT, preferred_element_type=F32
        ).astype(BF16)
        for block in range(4):
            partial[group, block] = product[:, block * TOK : (block + 1) * TOK]
        for dy in (1, 3, 2):
            remote(
                partial.at[group, ys[dy]], landed.at[dy - 1, group], 5, part_sems.at[dy - 1, group], dy=dy
            )

    def collect(group):
        total = partial[group, ys[0]].astype(F32)
        for dy in (1, 2, 3):
            arrival(landed.at[dy - 1, group], part_sems.at[dy - 1, group])
            total = total + landed[dy - 1, group].astype(F32)
        out[column(group)] = total.astype(BF16)

    sideways(0)
    sideways(1)
    relay(0)
    sideways(3)
    relay(1)
    sideways(2)
    relay(3)
    own[1].wait()
    for dz in (1, 3, 2):
        arrival(heads.at[:, lanes(dz)], head_sems.at[dz])
    multiply(0)
    multiply(1)
    relay(2)
    multiply(2)
    multiply(6)
    far(0)
    far(1)
    multiply(3)
    multiply(7)
    far(3)
    far(2)
    multiply(4)
    collect(0)
    collect(1)
    multiply(5)
    for group in (2, 6, 3, 7, 4, 5):
        collect(group)

    for index, sent in enumerate((
        wide.at[0, :, pl.ds(0, 3 * HEAD)],
        heads.at[:, pl.ds(0, 3 * HEAD)],
        wide.at[pl.ds(0, 4)],
        wide.at[pl.ds(0, 2)],
        wide.at[0],
        landed,
    )):
        arrival(sent, send_sems.at[index])


def project(attention, out_weight):
    anywhere = pl.BlockSpec(memory_space=pl.ANY)
    return pl.pallas_call(
        project_kernel,
        out_shape=jax.ShapeDtypeStruct((8, COLS, TOK), BF16),
        in_specs=[anywhere] * 2,
        out_specs=pl.BlockSpec(memory_space=pltpu.VMEM),
        scratch_shapes=[
            pltpu.VMEM((SPAN, 4 * HEAD), BF16),
            pltpu.VMEM((8, COLS, 4 * HEAD), BF16),
            pltpu.VMEM((8, 4, COLS, TOK), BF16),
            pltpu.VMEM((3, 8, COLS, TOK), BF16),
            pltpu.SemaphoreType.DMA((2,)),
            pltpu.SemaphoreType.DMA((4,)),
            pltpu.SemaphoreType.DMA((4, 8)),
            pltpu.SemaphoreType.DMA((4,)),
            pltpu.SemaphoreType.DMA((3, 8)),
            pltpu.SemaphoreType.DMA((4,)),
            pltpu.SemaphoreType.DMA((6,)),
        ],
        compiler_params=pltpu.CompilerParams(
            vmem_limit_bytes=VMEM, collective_id=1, has_side_effects=True
        ),
    )(attention[0], jnp.swapaxes(out_weight, 0, 1))

def unpack(mixer, messages):
    flat = messages.reshape(BLOCK * ROWS, SLICE)
    sorted_rows = jnp.dot(mixer, flat, preferred_element_type=F32).astype(BF16)
    return [sorted_rows[piece * BROWS : (piece + 1) * BROWS] for piece in range(PIECES)]


def pack(mixer_t, rows):
    stacked = jnp.concatenate(
        [rows[:, piece * SLICE : (piece + 1) * SLICE] for piece in range(PIECES)], axis=0
    )
    mixed = jnp.dot(mixer_t, stacked, preferred_element_type=F32).astype(BF16)
    return mixed.reshape(BLOCK, ROWS, SLICE)


def mixers():
    count = BLOCK * ROWS
    place = jnp.arange(count, dtype=I32)
    piece, position, message = place // BROWS, (place // BLOCK) % CAP, place % BLOCK
    source = message * ROWS + piece * CAP + position
    mixer = (source[:, None] == place[None, :]).astype(BF16)
    mixer_t = (place[:, None] == source[None, :]).astype(BF16)
    return mixer, mixer_t


def slot_columns():
    column = jnp.arange(DEV * CAP, dtype=I32)
    block, position, message = column // BROWS, (column // BLOCK) % CAP, column % BLOCK
    slot = block * BLOCK + message
    group, rest = slot // GROUP, slot % GROUP
    dz, dy, dc = rest // 8, (rest // 2) % 4, rest % 2
    dx = (group + 8 - dz - dy) % 4
    ctx, exp = lax.axis_index("ctx"), lax.axis_index("exp")
    ctx = (ctx // 4 + dz) % 4 * 4 + (ctx % 4 + dy) % 4
    exp = (exp // 2 + dx) % 4 * 2 + (exp % 2 + dc) % 2
    shape = (GROUPS, 1, GROWS)
    return (ctx * 8 + exp).astype(I32).reshape(shape), position.reshape(shape)


def pieces():
    return [(start, min(start + SLICE, D)) for start in range(0, D, SLICE)]


def moe_kernel(
    projected, gain, routes, gate_fixed, expert_col, position_col, mixer, mixer_t,
    w_gate, w_up, w_down,
    out,
    gate, up, down, send, landed, returned, arrived, activated, outputs, normed,
    chooser, shares, totals,
    weight_sems, send_sem, land_sems, result_sem, return_sems,
):
    loads = [
        pltpu.make_async_copy(source.at[0], target, weight_sems.at[i])
        for i, (source, target) in enumerate(((w_gate, gate), (w_up, up), (w_down, down)))
    ]
    for load in loads:
        load.start()
    zs, ys, xs, cores = ahead()

    def each(group, back, act):
        shift = 4 - group if back else group + 4
        across = [lax.rem(xs[0] + shift + (step if back else 4 - step), 4) for step in range(4)]
        for dz in range(4):
            for dy in range(4):
                for dc in range(2):
                    z, y = (zs[-dz % 4], ys[-dy % 4]) if back else (zs[dz], ys[dy])
                    target = (z * 4 + y, across[(dz + dy) % 4] * 2 + cores[dc])
                    slot = group * GROUP + dz * 8 + dy * 2 + dc
                    if dz + dy + dc:
                        act(slot, target)
                    else:
                        pl.when(group > 0)(lambda: act(slot, target))

    barrier = pltpu.get_barrier_semaphore()

    @pl.loop(0, GROUPS)
    def _(group):
        each(group, False, lambda slot, target: pl.semaphore_signal(
            barrier, inc=1, device_id=target, device_id_type=MESH))

    squares = jnp.zeros((1, TOK), F32)
    for start, stop in pieces():
        widened = projected[start:stop, :].astype(F32)
        squares = squares + jnp.sum(widened * widened, axis=0, keepdims=True)
    scale = lax.rsqrt(squares / D + 1e-05)
    normed[:, D:] = jnp.zeros((TOK, WIDE - D), BF16)
    outputs[:, D:] = jnp.zeros((GROWS, WIDE - D), BF16)
    for start, stop in pieces():
        scaled = jnp.transpose(projected[start:stop, :].astype(F32) * scale)
        normed[:, start:stop] = (scaled * gain[:, start:stop]).astype(BF16)
    earlier = lax.broadcasted_iota(I32, (TOK, TOK), 1) < lax.broadcasted_iota(I32, (TOK, TOK), 0)
    earlier = jnp.where(earlier, 1.0, 0.0).astype(BF16)

    @pl.loop(0, GROUPS)
    def _(group):
        fixed = jnp.zeros((TOK, GROWS), I32)
        for k in range(4):
            named = routes[:, k : k + 1] == expert_col[group]
            fixed = fixed + jnp.where(named, gate_fixed[:, k : k + 1], 0)
        chosen = jnp.where(fixed > 0, 1.0, 0.0)
        rank = jnp.dot(earlier, chosen.astype(BF16), preferred_element_type=F32)
        mask = (fixed > 0) & (rank == position_col[group].astype(F32))
        fixed = jnp.where(mask, fixed, 0)
        shares[group, :TOK] = (fixed >> 8).astype(F32).astype(BF16)
        shares[group, TOK:] = (fixed & 255).astype(F32).astype(BF16)
        chooser[group] = jnp.transpose(jnp.where(mask, 1.0, 0.0)).astype(BF16)

    pl.semaphore_wait(barrier, DEV - 1)

    def block_rows(block):
        return pl.ds(pl.multiple_of(block * BROWS, BROWS), BROWS)

    @pl.loop(0, GROUPS)
    def _(group):
        first = group * GROUP
        for piece in range(PIECES):
            columns = pl.ds(piece * SLICE, SLICE)
            arrived[:, columns] = jnp.dot(
                chooser[group], normed[:, columns], preferred_element_type=F32
            ).astype(BF16)

        @pl.loop(0, GROUP // BLOCK)
        def _(block):
            send[pl.ds(first + block * BLOCK, BLOCK)] = pack(mixer_t[...], arrived[block_rows(block), :])

        @pl.when(group == 0)
        def _():
            pltpu.make_async_copy(send.at[0], landed.at[0], land_sems.at[0]).start()

        each(group, False, lambda slot, target: pltpu.make_async_remote_copy(
            src_ref=send.at[slot], dst_ref=landed.at[slot], send_sem=send_sem,
            recv_sem=land_sems.at[group], device_id=target, device_id_type=MESH,
        ).start())

    for load in loads:
        load.wait()

    @pl.loop(0, GROUPS)
    def _(group):
        first = group * GROUP
        span = landed.at[pl.ds(first, GROUP)]
        pltpu.make_async_copy(span, span, land_sems.at[group]).wait()

        @pl.loop(0, GROUP // BLOCK)
        def _(block):
            rows = unpack(mixer[...], landed[pl.ds(first + block * BLOCK, BLOCK)])
            for piece in range(PIECES):
                arrived[block_rows(block), piece * SLICE : (piece + 1) * SLICE] = rows[piece]

        def hidden(start, count):
            units = pl.ds(start, count)
            gate_value = lax.dot_general(arrived[:, :D], gate[units, :], NT, preferred_element_type=F32)
            up_value = lax.dot_general(arrived[:, :D], up[units, :], NT, preferred_element_type=F32)
            activated[:, units] = (
                gate_value / (1.0 + jnp.exp(-1.702 * gate_value)) * (up_value + 1.0)
            ).astype(BF16)

        @pl.loop(0, FFW // 256)
        def _(tile):
            hidden(pl.multiple_of(tile * 256, 256), 256)

        hidden(FFW // 256 * 256, FFW % 256)

        def result(start, count):
            columns = pl.ds(start, count)
            outputs[:, columns] = jnp.dot(
                activated[...], down[:, columns], preferred_element_type=F32
            ).astype(BF16)

        @pl.loop(0, D // 256)
        def _(tile):
            result(pl.multiple_of(tile * 256, 256), 256)

        result(D // 256 * 256, D % 256)

        @pl.loop(0, GROUP // BLOCK)
        def _(block):
            landed[pl.ds(first + block * BLOCK, BLOCK)] = pack(mixer_t[...], outputs[block_rows(block), :])

        @pl.when(group == 0)
        def _():
            pltpu.make_async_copy(landed.at[0], returned.at[0], return_sems.at[0]).start()

        each(group, True, lambda slot, target: pltpu.make_async_remote_copy(
            src_ref=landed.at[slot], dst_ref=returned.at[slot], send_sem=result_sem,
            recv_sem=return_sems.at[group], device_id=target, device_id_type=MESH,
        ).start())

    totals[...] = jnp.zeros(totals.shape, F32)

    @pl.loop(0, GROUPS)
    def _(group):
        first = group * GROUP
        span = returned.at[pl.ds(first, GROUP)]
        pltpu.make_async_copy(span, span, return_sems.at[group]).wait()

        @pl.loop(0, GROUP // BLOCK)
        def _(block):
            rows = unpack(mixer[...], returned[pl.ds(first + block * BLOCK, BLOCK)])
            for piece in range(PIECES):
                arrived[block_rows(block), piece * SLICE : (piece + 1) * SLICE] = rows[piece]

        for start, stop in pieces():
            totals[:, start:stop] += jnp.dot(
                shares[group], arrived[:, start:stop], preferred_element_type=F32
            )

    for start, stop in pieces():
        combined = totals[:TOK, start:stop] * (1.0 / 256.0) + totals[TOK:, start:stop] * (1.0 / 65536.0)
        layer_out = projected[start:stop, :].astype(F32) + jnp.transpose(combined)
        out[start:stop, :] = layer_out.astype(BF16)

    sent = returned.at[pl.ds(1, DEV - 1)]
    pltpu.make_async_copy(sent, sent, send_sem).wait()
    pltpu.make_async_copy(sent, sent, result_sem).wait()


def moe(projected, gain, routes, gate_fixed, w_gate, w_up, w_down):
    near, anywhere = pl.BlockSpec(memory_space=pltpu.VMEM), pl.BlockSpec(memory_space=pl.ANY)
    message = pltpu.VMEM((DEV, ROWS, SLICE), BF16)
    return pl.pallas_call(
        moe_kernel,
        out_shape=jax.ShapeDtypeStruct((D, TOK), BF16),
        in_specs=[near] * 8 + [anywhere] * 3,
        out_specs=near,
        scratch_shapes=[
            pltpu.VMEM((FFW, D), BF16),
            pltpu.VMEM((FFW, D), BF16),
            pltpu.VMEM((FFW, D), BF16),
            message,
            message,
            message,
            pltpu.VMEM((GROWS, WIDE), BF16),
            pltpu.VMEM((GROWS, FFW), BF16),
            pltpu.VMEM((GROWS, WIDE), BF16),
            pltpu.VMEM((TOK, WIDE), BF16),
            pltpu.VMEM((GROUPS, GROWS, TOK), BF16),
            pltpu.VMEM((GROUPS, 2 * TOK, GROWS), BF16),
            pltpu.VMEM((2 * TOK, D), F32),
            pltpu.SemaphoreType.DMA((3,)),
            pltpu.SemaphoreType.DMA,
            pltpu.SemaphoreType.DMA((GROUPS,)),
            pltpu.SemaphoreType.DMA,
            pltpu.SemaphoreType.DMA((GROUPS,)),
        ],
        compiler_params=pltpu.CompilerParams(
            vmem_limit_bytes=VMEM, collective_id=0, has_side_effects=True
        ),
    )(
        projected, gain.reshape(1, D), routes, gate_fixed, *slot_columns(), *mixers(),
        jnp.swapaxes(w_gate, 1, 2), jnp.swapaxes(w_up, 1, 2), w_down,
    )


def shards(attention, out_weight, norm_gain, w_gate, w_up, w_down, routes, gate_fixed):
    projected = project(attention, out_weight).reshape(D, TOK)
    layer_out = moe(projected, norm_gain, routes[0], gate_fixed[0], w_gate, w_up, w_down)
    return jnp.swapaxes(layer_out, 0, 1)[None]


def solution(mesh):
    in_specs = (
        P("exp", None, "ctx"),
        P("ctx", "exp"),
        P(),
        P(("ctx", "exp"), None, None),
        P(("ctx", "exp"), None, None),
        P(("ctx", "exp"), None, None),
        P("exp", "ctx", None),
        P("exp", "ctx", None),
    )
    out_specs = P("exp", "ctx", None)
    return jax.shard_map(shards, mesh=mesh, in_specs=in_specs, out_specs=out_specs, check_vma=False)
```

```python
import jax
import jax.numpy as jnp
from jax import lax
from jax.experimental import pallas as pl
from jax.experimental.pallas import tpu as pltpu
from jax.sharding import PartitionSpec as P

MESH = pl.DeviceIdType.MESH
BF16, F32, I32 = jnp.bfloat16, jnp.float32, jnp.int32
NT = (((1,), (1,)), ((), ()))

D = 2880
FFW = 1440
TOK = 128
HEAD = 256
COLS = 360
SPAN = 4 * TOK
CAP = 6
DEV = 128
SLICE = 384
PIECES = 8
WIDE = SLICE * PIECES
ROWS = PIECES * CAP
BLOCK = 8
BROWS = BLOCK * CAP
GROUP = 32
GROUPS = DEV // GROUP
GROWS = GROUP * CAP
VMEM = 60 * 1024 * 1024


def ahead():
    ctx, exp = lax.axis_index("ctx"), lax.axis_index("exp")
    z, y = lax.div(ctx, 4), lax.rem(ctx, 4)
    x, core = lax.div(exp, 2), lax.rem(exp, 2)
    zs = [lax.rem(z + step, 4) for step in range(4)]
    ys = [lax.rem(y + step, 4) for step in range(4)]
    xs = [lax.rem(x + step, 4) for step in range(4)]
    cores = [core, 1 - core]
    return zs, ys, xs, cores


def project_kernel(
    attention, weight, out, heads, wide, partial, landed, hop,
    own_sems, head_sems, wide_sems, half_sems, part_sems, hop_sems, send_sems,
):
    zs, ys, xs, cores = ahead()

    def device(dz=0, dy=0, dx=0, dc=0):
        return zs[dz] * 4 + ys[dy], xs[dx] * 2 + cores[dc]

    def lanes(dz, start=0, count=HEAD):
        return pl.ds(dz * HEAD + start, count)

    def remote(source, target, send, receive, **offset):
        pltpu.make_async_remote_copy(
            src_ref=source, dst_ref=target, send_sem=send_sems.at[send], recv_sem=receive,
            device_id=device(**offset), device_id_type=MESH,
        ).start()

    def arrival(target, semaphore):
        pltpu.make_async_copy(target, target, semaphore).wait()

    def tokens(dz, dy):
        return attention.at[pl.ds(pl.multiple_of(zs[dz] * SPAN + ys[dy] * TOK, TOK), TOK)]

    def head_block(dz, dy):
        return heads.at[pl.ds(dy * TOK, TOK), lanes(dz)]

    own = [pltpu.make_async_copy(weight, wide.at[0, :, lanes(0)], own_sems.at[4])]
    own = [
        pltpu.make_async_copy(tokens(0, dy), head_block(0, dy), own_sems.at[dy]) for dy in range(4)
    ] + own
    for copy in own:
        copy.start()
    barrier = pltpu.get_barrier_semaphore()
    friends = (
        [dict(dz=d) for d in (1, 2, 3)] + [dict(dy=d) for d in (1, 3)]
        + [dict(dx=1), dict(dx=3), dict(dc=1)]
    )
    for offset in friends:
        pl.semaphore_signal(barrier, inc=1, device_id=device(**offset), device_id_type=MESH)
    pl.semaphore_wait(barrier, len(friends))

    for dz in (1, 3, 2):
        remote(weight, wide.at[0, :, lanes(dz)], 0, wide_sems.at[dz, 0], dz=dz)

    def across(dz, dx):
        slot = wide.at[2 * dx, :, lanes(dz)]
        remote(slot, wide.at[2 * dx + 1, :, lanes(dz)], 2, wide_sems.at[dz, 2 * dx + 1], dc=1)

    def sideways(dz):
        slot = wide.at[0, :, lanes(dz)]
        if dz:
            arrival(slot, wide_sems.at[dz, 0])
        else:
            own[4].wait()
        for dx in (1, 3):
            remote(slot, wide.at[2 * dx, :, lanes(dz)], 3, wide_sems.at[dz, 2 * dx], dx=dx)
        across(dz, 0)

    def relay(dz):
        for dx, start, semaphore in ((1, 0, wide_sems.at[dz, 4]), (3, 128, half_sems.at[dz])):
            arrival(wide.at[2 * dx, :, lanes(dz)], wide_sems.at[dz, 2 * dx])
            remote(
                wide.at[2 * dx, :, lanes(dz, start, 128)], wide.at[4, :, lanes(dz, start, 128)],
                4, semaphore, dx=dx,
            )
            across(dz, dx)

    def far(dz):
        arrival(wide.at[4, :, lanes(dz, 0, 128)], wide_sems.at[dz, 4])
        arrival(wide.at[4, :, lanes(dz, 128, 128)], half_sems.at[dz])
        across(dz, 2)

    def ready(group):
        if group % 2:
            for dz in range(4):
                arrival(wide.at[group, :, lanes(dz)], wide_sems.at[dz, group])

    def ready_heads(dy):
        own[dy].wait()
        for dz in (1, 3, 2):
            arrival(head_block(dz, dy), head_sems.at[dz, dy])

    def multiply(group, blocks):
        rows = heads[blocks[0] * TOK : (blocks[-1] + 1) * TOK, :]
        product = lax.dot_general(wide[group], rows, NT, preferred_element_type=F32).astype(BF16)
        for place, dy in enumerate(blocks):
            partial[group, dy] = product[:, place * TOK : (place + 1) * TOK]

    def via(group):
        return 3 if group % 2 else 1

    def send_hop(group):
        remote(partial.at[group, 2], hop.at[group], 5, hop_sems.at[group], dy=via(group))

    def send_plain(group):
        dy = 4 - via(group)
        remote(partial.at[group, dy], landed.at[dy // 2, group], 5, part_sems.at[dy // 2, group], dy=dy)

    def send_joined(group):
        dy = via(group)
        arrival(hop.at[group], hop_sems.at[group])
        partial[group, dy] = (partial[group, dy].astype(F32) + hop[group].astype(F32)).astype(BF16)
        remote(partial.at[group, dy], landed.at[dy // 2, group], 5, part_sems.at[dy // 2, group], dy=dy)

    def collect(group):
        total = partial[group, 0].astype(F32)
        for side in range(2):
            arrival(landed.at[side, group], part_sems.at[side, group])
            total = total + landed[side, group].astype(F32)
        out[xs[(4 - group // 2) % 4] * 2 + cores[group % 2]] = total.astype(BF16)

    sideways(0)
    for dy in (2, 3, 1, 0):
        for dz in (1, 3, 2):
            remote(tokens(dz, dy), head_block(dz, dy), 1, head_sems.at[dz, dy], dz=dz)
    sideways(1)
    relay(0)
    sideways(3)
    relay(1)
    sideways(2)
    ready_heads(2)
    multiply(0, (2,))
    send_hop(0)
    relay(3)
    ready(1)
    multiply(1, (2,))
    send_hop(1)
    ready_heads(3)
    multiply(0, (3,))
    send_plain(0)
    relay(2)
    multiply(1, (3,))
    ready_heads(1)
    multiply(1, (1,))
    send_plain(1)
    multiply(0, (1,))
    send_joined(0)
    send_joined(1)
    ready_heads(0)
    multiply(0, (0,))
    multiply(1, (0,))
    previous = None
    for group in (2, 6, 3, 7, 4, 5):
        if group == 3:
            far(0)
            far(1)
        if group == 4:
            far(3)
            far(2)
        ready(group)
        multiply(group, (0, 1, 2, 3))
        send_hop(group)
        send_plain(group)
        if previous is not None:
            send_joined(previous)
        previous = group
    send_joined(previous)
    for group in (0, 1, 2, 6, 3, 7, 4, 5):
        collect(group)

    for index, sent in enumerate((
        wide.at[0, :, pl.ds(0, 3 * HEAD)],
        heads.at[:, pl.ds(0, 3 * HEAD)],
        wide.at[pl.ds(0, 4)],
        wide.at[pl.ds(0, 2)],
        wide.at[0],
        partial.at[:, pl.ds(0, 3)],
    )):
        arrival(sent, send_sems.at[index])


def project(attention, out_weight):
    anywhere = pl.BlockSpec(memory_space=pl.ANY)
    return pl.pallas_call(
        project_kernel,
        out_shape=jax.ShapeDtypeStruct((8, COLS, TOK), BF16),
        in_specs=[anywhere] * 2,
        out_specs=pl.BlockSpec(memory_space=pltpu.VMEM),
        scratch_shapes=[
            pltpu.VMEM((SPAN, 4 * HEAD), BF16),
            pltpu.VMEM((8, COLS, 4 * HEAD), BF16),
            pltpu.VMEM((8, 4, COLS, TOK), BF16),
            pltpu.VMEM((2, 8, COLS, TOK), BF16),
            pltpu.VMEM((8, COLS, TOK), BF16),
            pltpu.SemaphoreType.DMA((5,)),
            pltpu.SemaphoreType.DMA((4, 4)),
            pltpu.SemaphoreType.DMA((4, 8)),
            pltpu.SemaphoreType.DMA((4,)),
            pltpu.SemaphoreType.DMA((2, 8)),
            pltpu.SemaphoreType.DMA((8,)),
            pltpu.SemaphoreType.DMA((6,)),
        ],
        compiler_params=pltpu.CompilerParams(
            vmem_limit_bytes=VMEM, collective_id=1, has_side_effects=True
        ),
    )(attention[0], jnp.swapaxes(out_weight, 0, 1))

def unpack(mixer, messages):
    flat = messages.reshape(BLOCK * ROWS, SLICE)
    sorted_rows = jnp.dot(mixer, flat, preferred_element_type=F32).astype(BF16)
    return [sorted_rows[piece * BROWS : (piece + 1) * BROWS] for piece in range(PIECES)]


def pack(mixer_t, rows):
    stacked = jnp.concatenate(
        [rows[:, piece * SLICE : (piece + 1) * SLICE] for piece in range(PIECES)], axis=0
    )
    mixed = jnp.dot(mixer_t, stacked, preferred_element_type=F32).astype(BF16)
    return mixed.reshape(BLOCK, ROWS, SLICE)


def sixth(value):
    whole = (value * 43) >> 8
    return whole, value - 6 * whole


def mixed_places(place):
    piece, position = sixth(place >> 3)
    return (place & 7) * ROWS + piece * CAP + position


def write_mixers(mixer, mixer_t):
    count = BLOCK * ROWS
    source = mixed_places(lax.broadcasted_iota(I32, (count, count), 0))
    place = lax.broadcasted_iota(I32, (count, count), 1)
    mixer[...] = jnp.where(source == place, 1.0, 0.0).astype(BF16)
    source = mixed_places(place)
    place = lax.broadcasted_iota(I32, (count, count), 0)
    mixer_t[...] = jnp.where(source == place, 1.0, 0.0).astype(BF16)


def slot_columns(group, zs, ys, xs, cores):
    column = lax.broadcasted_iota(I32, (1, GROWS), 1)
    dz, position = sixth(column >> 3)
    dy, dc = (column & 7) >> 1, column & 1
    dx = (group + 8 - dz - dy) & 3
    z, y = (zs[0] + dz) & 3, (ys[0] + dy) & 3
    x, core = (xs[0] + dx) & 3, (cores[0] + dc) & 1
    return (z * 4 + y) * 8 + x * 2 + core, position


def pieces():
    return [(start, min(start + SLICE, D)) for start in range(0, D, SLICE)]


def moe_kernel(
    projected, gain, routes, gate_fixed, w_gate, w_up, w_down,
    out,
    gate, up, down, send, landed, returned, arrived, activated, outputs, normed,
    chooser, shares, totals, mixer, mixer_t,
    weight_sems, send_sem, land_sems, result_sem, return_sems, round_sems,
):
    loads = [
        pltpu.make_async_copy(source.at[0], target, weight_sems.at[i])
        for i, (source, target) in enumerate(((w_gate, gate), (w_up, up), (w_down, down)))
    ]
    for load in loads:
        load.start()
    zs, ys, xs, cores = ahead()

    def each(group, back, act):
        shift = 4 - group if back else group + 4
        across = [lax.rem(xs[0] + shift + (step if back else 4 - step), 4) for step in range(4)]
        for dz in range(4):
            for dy in range(4):
                for dc in range(2):
                    z, y = (zs[-dz % 4], ys[-dy % 4]) if back else (zs[dz], ys[dy])
                    target = (z * 4 + y, across[(dz + dy) % 4] * 2 + cores[dc])
                    slot = group * GROUP + dz * 8 + dy * 2 + dc
                    if dz + dy + dc:
                        act(slot, target)
                    else:
                        pl.when(group > 0)(lambda: act(slot, target))

    lines = {
        "z": [(zs[d] * 4 + ys[0], xs[0] * 2 + cores[0]) for d in (1, 2, 3)],
        "y": [(zs[0] * 4 + ys[d], xs[0] * 2 + cores[0]) for d in (1, 2, 3)],
        "x": [(zs[0] * 4 + ys[0], xs[d] * 2 + cores[c]) for d in range(4) for c in range(2) if d + c],
    }

    def greet(semaphore, line):
        for target in lines[line]:
            pl.semaphore_signal(semaphore, inc=1, device_id=target, device_id_type=MESH)

    barrier = pltpu.get_barrier_semaphore()
    for line in lines:
        greet(barrier, line)
    write_mixers(mixer, mixer_t)
    pl.semaphore_wait(barrier, sum(len(line) for line in lines.values()))
    greet(round_sems.at[0], "y")

    squares = jnp.zeros((1, TOK), F32)
    for start, stop in pieces():
        widened = projected[start:stop, :].astype(F32)
        squares = squares + jnp.sum(widened * widened, axis=0, keepdims=True)
    scale = lax.rsqrt(squares / D + 1e-05)
    normed[:, D:] = jnp.zeros((TOK, WIDE - D), BF16)
    outputs[:, D:] = jnp.zeros((GROWS, WIDE - D), BF16)
    for start, stop in pieces():
        scaled = jnp.transpose(projected[start:stop, :].astype(F32) * scale)
        normed[:, start:stop] = (scaled * gain[start:stop].reshape(1, stop - start)).astype(BF16)
    pl.semaphore_wait(round_sems.at[0], len(lines["y"]))
    greet(round_sems.at[1], "x")
    earlier = lax.broadcasted_iota(I32, (TOK, TOK), 1) < lax.broadcasted_iota(I32, (TOK, TOK), 0)
    earlier = jnp.where(earlier, 1.0, 0.0).astype(BF16)

    named_experts = jnp.transpose(routes[...])
    named_shares = jnp.transpose(gate_fixed[...])

    @pl.loop(0, GROUPS)
    def _(group):
        expert, position = slot_columns(group, zs, ys, xs, cores)
        fixed = jnp.zeros((TOK, GROWS), I32)
        for k in range(4):
            named = named_experts[:, k : k + 1] == expert
            fixed = fixed + jnp.where(named, named_shares[:, k : k + 1], 0)
        chosen = jnp.where(fixed > 0, 1.0, 0.0)
        rank = jnp.dot(earlier, chosen.astype(BF16), preferred_element_type=F32)
        mask = (fixed > 0) & (rank == position.astype(F32))
        fixed = jnp.where(mask, fixed, 0)
        shares[group, :TOK] = (fixed >> 8).astype(F32).astype(BF16)
        shares[group, TOK:] = (fixed & 255).astype(F32).astype(BF16)
        chooser[group] = jnp.transpose(jnp.where(mask, 1.0, 0.0)).astype(BF16)

    pl.semaphore_wait(round_sems.at[1], len(lines["x"]))

    def block_rows(block):
        return pl.ds(pl.multiple_of(block * BROWS, BROWS), BROWS)

    @pl.loop(0, GROUPS)
    def _(group):
        first = group * GROUP
        for piece in range(PIECES):
            columns = pl.ds(piece * SLICE, SLICE)
            arrived[:, columns] = jnp.dot(
                chooser[group], normed[:, columns], preferred_element_type=F32
            ).astype(BF16)

        @pl.loop(0, GROUP // BLOCK)
        def _(block):
            send[pl.ds(first + block * BLOCK, BLOCK)] = pack(mixer_t[...], arrived[block_rows(block), :])

        @pl.when(group == 0)
        def _():
            pltpu.make_async_copy(send.at[0], landed.at[0], land_sems.at[0]).start()

        each(group, False, lambda slot, target: pltpu.make_async_remote_copy(
            src_ref=send.at[slot], dst_ref=landed.at[slot], send_sem=send_sem,
            recv_sem=land_sems.at[group], device_id=target, device_id_type=MESH,
        ).start())

    for load in loads:
        load.wait()

    @pl.loop(0, GROUPS)
    def _(group):
        first = group * GROUP
        span = landed.at[pl.ds(first, GROUP)]
        pltpu.make_async_copy(span, span, land_sems.at[group]).wait()

        @pl.loop(0, GROUP // BLOCK)
        def _(block):
            rows = unpack(mixer[...], landed[pl.ds(first + block * BLOCK, BLOCK)])
            for piece in range(PIECES):
                arrived[block_rows(block), piece * SLICE : (piece + 1) * SLICE] = rows[piece]

        def hidden(start, count):
            units = pl.ds(start, count)
            gate_value = lax.dot_general(arrived[:, :D], gate[units, :], NT, preferred_element_type=F32)
            up_value = lax.dot_general(arrived[:, :D], up[units, :], NT, preferred_element_type=F32)
            activated[:, units] = (
                gate_value / (1.0 + jnp.exp(-1.702 * gate_value)) * (up_value + 1.0)
            ).astype(BF16)

        @pl.loop(0, FFW // 256)
        def _(tile):
            hidden(pl.multiple_of(tile * 256, 256), 256)

        hidden(FFW // 256 * 256, FFW % 256)

        def result(start, count):
            columns = pl.ds(start, count)
            outputs[:, columns] = jnp.dot(
                activated[...], down[:, columns], preferred_element_type=F32
            ).astype(BF16)

        @pl.loop(0, D // 256)
        def _(tile):
            result(pl.multiple_of(tile * 256, 256), 256)

        result(D // 256 * 256, D % 256)

        @pl.loop(0, GROUP // BLOCK)
        def _(block):
            landed[pl.ds(first + block * BLOCK, BLOCK)] = pack(mixer_t[...], outputs[block_rows(block), :])

        @pl.when(group == 0)
        def _():
            pltpu.make_async_copy(landed.at[0], returned.at[0], return_sems.at[0]).start()

        each(group, True, lambda slot, target: pltpu.make_async_remote_copy(
            src_ref=landed.at[slot], dst_ref=returned.at[slot], send_sem=result_sem,
            recv_sem=return_sems.at[group], device_id=target, device_id_type=MESH,
        ).start())

    totals[...] = jnp.zeros(totals.shape, F32)

    @pl.loop(0, GROUPS)
    def _(group):
        first = group * GROUP
        span = returned.at[pl.ds(first, GROUP)]
        pltpu.make_async_copy(span, span, return_sems.at[group]).wait()

        @pl.loop(0, GROUP // BLOCK)
        def _(block):
            rows = unpack(mixer[...], returned[pl.ds(first + block * BLOCK, BLOCK)])
            for piece in range(PIECES):
                arrived[block_rows(block), piece * SLICE : (piece + 1) * SLICE] = rows[piece]

        for start, stop in pieces():
            totals[:, start:stop] += jnp.dot(
                shares[group], arrived[:, start:stop], preferred_element_type=F32
            )

    for start, stop in pieces():
        combined = totals[:TOK, start:stop] * (1.0 / 256.0) + totals[TOK:, start:stop] * (1.0 / 65536.0)
        layer_out = projected[start:stop, :].astype(F32) + jnp.transpose(combined)
        out[start:stop, :] = layer_out.astype(BF16)

    sent = returned.at[pl.ds(1, DEV - 1)]
    pltpu.make_async_copy(sent, sent, send_sem).wait()
    pltpu.make_async_copy(sent, sent, result_sem).wait()


def moe(projected, gain, routes, gate_fixed, w_gate, w_up, w_down):
    near, anywhere = pl.BlockSpec(memory_space=pltpu.VMEM), pl.BlockSpec(memory_space=pl.ANY)
    message = pltpu.VMEM((DEV, ROWS, SLICE), BF16)
    return pl.pallas_call(
        moe_kernel,
        out_shape=jax.ShapeDtypeStruct((D, TOK), BF16),
        in_specs=[near] * 4 + [anywhere] * 3,
        out_specs=near,
        scratch_shapes=[
            pltpu.VMEM((FFW, D), BF16),
            pltpu.VMEM((FFW, D), BF16),
            pltpu.VMEM((FFW, D), BF16),
            message,
            message,
            message,
            pltpu.VMEM((GROWS, WIDE), BF16),
            pltpu.VMEM((GROWS, FFW), BF16),
            pltpu.VMEM((GROWS, WIDE), BF16),
            pltpu.VMEM((TOK, WIDE), BF16),
            pltpu.VMEM((GROUPS, GROWS, TOK), BF16),
            pltpu.VMEM((GROUPS, 2 * TOK, GROWS), BF16),
            pltpu.VMEM((2 * TOK, D), F32),
            pltpu.VMEM((BLOCK * ROWS, BLOCK * ROWS), BF16),
            pltpu.VMEM((BLOCK * ROWS, BLOCK * ROWS), BF16),
            pltpu.SemaphoreType.DMA((3,)),
            pltpu.SemaphoreType.DMA,
            pltpu.SemaphoreType.DMA((GROUPS,)),
            pltpu.SemaphoreType.DMA,
            pltpu.SemaphoreType.DMA((GROUPS,)),
            pltpu.SemaphoreType.REGULAR((2,)),
        ],
        compiler_params=pltpu.CompilerParams(
            vmem_limit_bytes=VMEM, collective_id=0, has_side_effects=True
        ),
    )(
        projected, gain, jnp.swapaxes(routes, 0, 1), jnp.swapaxes(gate_fixed, 0, 1),
        jnp.swapaxes(w_gate, 1, 2), jnp.swapaxes(w_up, 1, 2), w_down,
    )


def shards(attention, out_weight, norm_gain, w_gate, w_up, w_down, routes, gate_fixed):
    projected = project(attention, out_weight).reshape(D, TOK)
    layer_out = moe(projected, norm_gain, routes[0], gate_fixed[0], w_gate, w_up, w_down)
    return jnp.swapaxes(layer_out, 0, 1)[None]


def solution(mesh):
    in_specs = (
        P("exp", None, "ctx"),
        P("ctx", "exp"),
        P(),
        P(("ctx", "exp"), None, None),
        P(("ctx", "exp"), None, None),
        P(("ctx", "exp"), None, None),
        P("exp", "ctx", None),
        P("exp", "ctx", None),
    )
    out_specs = P("exp", "ctx", None)
    return jax.shard_map(shards, mesh=mesh, in_specs=in_specs, out_specs=out_specs, check_vma=False)
```

```python
import jax
import jax.numpy as jnp
import numpy as np
from jax import lax
from jax.experimental import pallas as pl
from jax.experimental.pallas import tpu as pltpu
from jax.sharding import PartitionSpec as P

MESH = pl.DeviceIdType.MESH
BF16, F32, I32 = jnp.bfloat16, jnp.float32, jnp.int32
NT = (((1,), (1,)), ((), ()))

D = 2880
FFW = 1440
TOK = 128
HEAD = 256
COLS = 360
SPAN = 4 * TOK
CAP = 6
DEV = 128
SLICE = 384
PIECES = 8
WIDE = SLICE * PIECES
ROWS = PIECES * CAP
BLOCK = 4
BROWS = BLOCK * CAP
LAYER = 8 // BLOCK
GROUP = 32
GROUPS = DEV // GROUP
GROWS = GROUP * CAP
LAYERS = GROUP // 8


def hops(offset):
    return sum(min(step, 4 - step) for step in offset[:3])


OFFSETS = sorted(
    ((dz, dy, dx, dc) for dz in range(4) for dy in range(4) for dx in range(4) for dc in range(2)),
    key=lambda offset: (hops(offset), (offset[0] * 5 + offset[1] * 3 + offset[2] * 7 + offset[3] * 4) % 11),
)
OWN = OFFSETS.index((0, 0, 0, 0))
VMEM = 62 * 1024 * 1024


def ahead():
    ctx, exp = lax.axis_index("ctx"), lax.axis_index("exp")
    z, y = lax.div(ctx, 4), lax.rem(ctx, 4)
    x, core = lax.div(exp, 2), lax.rem(exp, 2)
    zs = [lax.rem(z + step, 4) for step in range(4)]
    ys = [lax.rem(y + step, 4) for step in range(4)]
    xs = [lax.rem(x + step, 4) for step in range(4)]
    cores = [core, 1 - core]
    return zs, ys, xs, cores


def project(
    place, meanwhile, attention, weight, projected, heads, wide, partial, sums, hop,
    own_sems, head_sems, wide_sems, half_sems, part_sems, hop_sems, send_sems,
):
    zs, ys, xs, cores = place

    def device(dz=0, dy=0, dx=0, dc=0):
        return zs[dz] * 4 + ys[dy], xs[dx] * 2 + cores[dc]

    def lanes(dz, start=0, count=HEAD):
        return pl.ds(dz * HEAD + start, count)

    def remote(source, target, send, receive, **offset):
        pltpu.make_async_remote_copy(
            src_ref=source, dst_ref=target, send_sem=send_sems.at[send], recv_sem=receive,
            device_id=device(**offset), device_id_type=MESH,
        ).start()

    def arrival(target, semaphore):
        pltpu.make_async_copy(target, target, semaphore).wait()

    def tokens(dz, dy):
        return attention.at[pl.ds(pl.multiple_of(zs[dz] * SPAN + ys[dy] * TOK, TOK), TOK)]

    def head_block(dz, dy):
        return heads.at[pl.ds(dy * TOK, TOK), lanes(dz)]

    own = [pltpu.make_async_copy(weight, wide.at[0, :, lanes(0)], own_sems.at[4])]
    own = [
        pltpu.make_async_copy(tokens(0, dy), head_block(0, dy), own_sems.at[dy]) for dy in range(4)
    ] + own
    for copy in own:
        copy.start()
    barrier = pltpu.get_barrier_semaphore()
    friends = (
        [dict(dz=d) for d in (1, 2, 3)] + [dict(dy=d) for d in (1, 3)]
        + [dict(dx=1), dict(dx=3), dict(dc=1)]
    )
    for offset in friends:
        pl.semaphore_signal(barrier, inc=1, device_id=device(**offset), device_id_type=MESH)
    pl.semaphore_wait(barrier, len(friends))

    for dz in (1, 3, 2):
        remote(weight, wide.at[0, :, lanes(dz)], 0, wide_sems.at[dz, 0], dz=dz)

    def across(dz, dx):
        slot = wide.at[2 * dx, :, lanes(dz)]
        remote(slot, wide.at[2 * dx + 1, :, lanes(dz)], 2, wide_sems.at[dz, 2 * dx + 1], dc=1)

    def sideways(dz):
        slot = wide.at[0, :, lanes(dz)]
        if dz:
            arrival(slot, wide_sems.at[dz, 0])
        else:
            own[4].wait()
        for dx in (1, 3):
            remote(slot, wide.at[2 * dx, :, lanes(dz)], 3, wide_sems.at[dz, 2 * dx], dx=dx)
        across(dz, 0)

    def relay(dz):
        for dx, start, semaphore in ((1, 0, wide_sems.at[dz, 4]), (3, 128, half_sems.at[dz])):
            arrival(wide.at[2 * dx, :, lanes(dz)], wide_sems.at[dz, 2 * dx])
            remote(
                wide.at[2 * dx, :, lanes(dz, start, 128)], wide.at[4, :, lanes(dz, start, 128)],
                4, semaphore, dx=dx,
            )
            across(dz, dx)

    def far(dz):
        arrival(wide.at[4, :, lanes(dz, 0, 128)], wide_sems.at[dz, 4])
        arrival(wide.at[4, :, lanes(dz, 128, 128)], half_sems.at[dz])
        across(dz, 2)

    def ready(group):
        if group % 2:
            for dz in range(4):
                arrival(wide.at[group, :, lanes(dz)], wide_sems.at[dz, group])

    def ready_heads(dy):
        own[dy].wait()
        for dz in (1, 3, 2):
            arrival(head_block(dz, dy), head_sems.at[dz, dy])

    def multiply(group, blocks):
        rows = heads[blocks[0] * TOK : (blocks[-1] + 1) * TOK, :]
        product = lax.dot_general(wide[group], rows, NT, preferred_element_type=F32).astype(BF16)
        for place, dy in enumerate(blocks):
            partial[group, dy] = product[:, place * TOK : (place + 1) * TOK]

    def via(group):
        return 3 if group % 2 else 1

    def send_hop(group):
        remote(partial.at[group, 2], hop.at[group], 5, hop_sems.at[group], dy=via(group))

    def send_plain(group):
        dy = 4 - via(group)
        remote(partial.at[group, dy], sums.at[dy // 2, group], 5, part_sems.at[dy // 2, group], dy=dy)

    def send_joined(group):
        dy = via(group)
        arrival(hop.at[group], hop_sems.at[group])
        partial[group, dy] = (partial[group, dy].astype(F32) + hop[group].astype(F32)).astype(BF16)
        remote(partial.at[group, dy], sums.at[dy // 2, group], 5, part_sems.at[dy // 2, group], dy=dy)

    def collect(group):
        total = partial[group, 0].astype(F32)
        for side in range(2):
            arrival(sums.at[side, group], part_sems.at[side, group])
            total = total + sums[side, group].astype(F32)
        total = total.astype(BF16).astype(F32)
        column = xs[(4 - group // 2) % 4] * 2 + cores[group % 2]
        projected[pl.ds(pl.multiple_of(column * COLS, 8), COLS), :] = total
        return jnp.sum(total * total, axis=0, keepdims=True)

    sideways(0)
    for dy in (2, 3, 1, 0):
        for dz in (1, 3, 2):
            remote(tokens(dz, dy), head_block(dz, dy), 1, head_sems.at[dz, dy], dz=dz)
    sideways(1)
    relay(0)
    sideways(3)
    relay(1)
    sideways(2)
    meanwhile()
    ready_heads(2)
    multiply(0, (2,))
    send_hop(0)
    relay(3)
    ready(1)
    multiply(1, (2,))
    send_hop(1)
    ready_heads(3)
    multiply(0, (3,))
    send_plain(0)
    relay(2)
    multiply(1, (3,))
    ready_heads(1)
    multiply(1, (1,))
    send_plain(1)
    multiply(0, (1,))
    send_joined(0)
    send_joined(1)
    ready_heads(0)
    multiply(0, (0,))
    multiply(1, (0,))
    previous = None
    for group in (2, 6, 3, 7, 4, 5):
        if group == 3:
            far(0)
            far(1)
        if group == 4:
            far(3)
            far(2)
        ready(group)
        multiply(group, (0, 1, 2, 3))
        send_hop(group)
        send_plain(group)
        if previous is not None:
            send_joined(previous)
        previous = group
    send_joined(previous)
    squares = jnp.zeros((1, TOK), F32)
    for group in (0, 1, 2, 6, 3, 7, 4, 5):
        squares = squares + collect(group)
    sent = enumerate((
        wide.at[0, :, pl.ds(0, 3 * HEAD)],
        heads.at[:, pl.ds(0, 3 * HEAD)],
        wide.at[pl.ds(0, 4)],
        wide.at[pl.ds(0, 2)],
        wide.at[0],
        partial.at[:, pl.ds(0, 3)],
    ))
    return squares, lambda: [arrival(target, send_sems.at[index]) for index, target in sent]


def unpack(mixer, messages, rows, block):
    flat = messages.reshape(BLOCK * ROWS, SLICE)
    sorted_rows = jnp.dot(mixer, flat, preferred_element_type=F32).astype(BF16)
    for piece in range(PIECES):
        rows[block * BROWS : (block + 1) * BROWS, piece * SLICE : (piece + 1) * SLICE] = sorted_rows[
            piece * BROWS : (piece + 1) * BROWS
        ]


def pack(mixer_t, rows, block):
    stacked = jnp.concatenate(
        [
            rows[block * BROWS : (block + 1) * BROWS, piece * SLICE : (piece + 1) * SLICE]
            for piece in range(PIECES)
        ],
        axis=0,
    )
    mixed = jnp.dot(mixer_t, stacked, preferred_element_type=F32).astype(BF16)
    return mixed.reshape(BLOCK, ROWS, SLICE)


def sixth(value):
    whole = (value * 43) >> 8
    return whole, value - 6 * whole


def mixed_places(place):
    piece, position = sixth(place >> 2)
    return (place & 3) * ROWS + piece * CAP + position


def write_mixers(mixer, mixer_t):
    count = BLOCK * ROWS
    source = mixed_places(lax.broadcasted_iota(I32, (count, count), 0))
    place = lax.broadcasted_iota(I32, (count, count), 1)
    mixer[...] = jnp.where(source == place, 1.0, 0.0).astype(BF16)
    source = mixed_places(place)
    place = lax.broadcasted_iota(I32, (count, count), 0)
    mixer_t[...] = jnp.where(source == place, 1.0, 0.0).astype(BF16)


def slot_columns(offsets, zs, ys, xs, cores):
    position = sixth(lax.broadcasted_iota(I32, (1, GROWS), 1) >> 2)[1]
    dz, dy, dx, dc = offsets >> 5, (offsets >> 3) & 3, (offsets >> 1) & 3, offsets & 1
    z, y = (zs[0] + dz) & 3, (ys[0] + dy) & 3
    x, core = (xs[0] + dx) & 3, (cores[0] + dc) & 1
    return (z * 4 + y) * 8 + x * 2 + core, position


def row_offsets():
    row = np.arange(DEV * CAP)
    slot = row // BROWS * BLOCK + row % BLOCK
    numbers = np.array([dz * 32 + dy * 8 + dx * 2 + dc for dz, dy, dx, dc in OFFSETS], np.int32)
    return jnp.asarray(numbers[slot].reshape(GROUPS, 1, GROWS))


HALF = 1408


def pieces():
    return [(start, min(start + SLICE, D)) for start in range(0, D, SLICE)]


def layer_kernel(
    attention, out_weight, gain, routes, gate_fixed, row_offset, w_gate, w_up, w_down,
    out,
    projected, heads, wide, partial, sums, hop,
    own_sems, head_sems, wide_sems, half_sems, part_sems, hop_sems, part_send_sems,
    gate, up, down, send, landed, returned, arrived, activated, normed,
    chooser, shares, totals, mixer, mixer_t,
    weight_sems, send_sem, land_sems, result_sem, return_sems,
):
    loads = [
        pltpu.make_async_copy(source.at[0], target, weight_sems.at[i])
        for i, (source, target) in enumerate(((w_gate, gate), (w_up, up), (w_down, down)))
    ]
    place = ahead()
    zs, ys, xs, cores = place

    def each(group, back, act, layers=range(LAYERS)):
        sign = -1 if back else 1

        def some(first, count):
            for slot in range(first, first + count):
                dz, dy, dx, dc = OFFSETS[slot]
                if slot != OWN:
                    target = (
                        zs[sign * dz % 4] * 4 + ys[sign * dy % 4],
                        xs[sign * dx % 4] * 2 + cores[dc],
                    )
                    act(slot, target)

        for here in range(GROUPS):
            for layer in layers:
                pl.when(group == here)(lambda: some(here * GROUP + layer * 8, 8))

    def prepare():
        write_mixers(mixer, mixer_t)
        earlier = lax.broadcasted_iota(I32, (TOK, TOK), 1) < lax.broadcasted_iota(I32, (TOK, TOK), 0)
        earlier = jnp.where(earlier, 1.0, 0.0).astype(BF16)

        named_experts = jnp.transpose(routes[...])
        named_shares = jnp.transpose(gate_fixed[...])

        @pl.loop(0, GROUPS)
        def _(group):
            expert, position = slot_columns(row_offset[group], zs, ys, xs, cores)
            fixed = jnp.zeros((TOK, GROWS), I32)
            for k in range(4):
                named = named_experts[:, k : k + 1] == expert
                fixed = fixed + jnp.where(named, named_shares[:, k : k + 1], 0)
            chosen = jnp.where(fixed > 0, 1.0, 0.0)
            rank = jnp.dot(earlier, chosen.astype(BF16), preferred_element_type=F32)
            mask = (fixed > 0) & (rank == position.astype(F32))
            fixed = jnp.where(mask, fixed, 0)
            shares[group, :TOK] = (fixed >> 8).astype(F32).astype(BF16)
            shares[group, TOK:] = (fixed & 255).astype(F32).astype(BF16)
            chooser[group] = jnp.transpose(jnp.where(mask, 1.0, 0.0)).astype(BF16)

    squares, last_waits = project(
        place, prepare, attention, out_weight, projected, heads, wide, partial, sums, hop,
        own_sems, head_sems, wide_sems, half_sems, part_sems, hop_sems, part_send_sems,
    )
    for load in loads:
        load.start()
    scale = lax.rsqrt(squares / D + 1e-05)
    normed[:, D:] = jnp.zeros((TOK, WIDE - D), BF16)
    for start, stop in pieces():
        scaled = jnp.transpose(projected[start:stop, :] * scale)
        normed[:, start:stop] = (scaled * gain[start:stop].reshape(1, stop - start)).astype(BF16)

    @pl.loop(0, GROUPS)
    def _(group):
        first = group * GROUP
        for piece in range(PIECES):
            columns = pl.ds(piece * SLICE, SLICE)
            arrived[:, columns] = jnp.dot(
                chooser[group], normed[:, columns], preferred_element_type=F32
            ).astype(BF16)

        for layer in range(4):
            for block in range(layer * LAYER, layer * LAYER + LAYER):
                send[pl.ds(first + block * BLOCK, BLOCK)] = pack(mixer_t[...], arrived, block)
            if layer == OWN % GROUP // 8:
                @pl.when(group == OWN // GROUP)
                def _():
                    pltpu.make_async_copy(send.at[OWN], landed.at[OWN], land_sems.at[group]).start()

            each(group, False, lambda slot, target: pltpu.make_async_remote_copy(
                src_ref=send.at[slot], dst_ref=landed.at[slot], send_sem=send_sem,
                recv_sem=land_sems.at[group], device_id=target, device_id_type=MESH,
            ).start(), [layer])

    for load in loads:
        load.wait()

    @pl.loop(0, GROUPS)
    def _(group):
        first = group * GROUP
        span = landed.at[pl.ds(first, GROUP)]
        pltpu.make_async_copy(span, span, land_sems.at[group]).wait()

        for block in range(GROUP // BLOCK):
            unpack(mixer[...], landed[pl.ds(first + block * BLOCK, BLOCK)], arrived, block)

        gate_value = lax.dot_general(arrived[:, :D], gate[...], NT, preferred_element_type=F32)
        up_value = lax.dot_general(arrived[:, :D], up[...], NT, preferred_element_type=F32)
        activated[...] = (
            gate_value / (1.0 + jnp.exp(-1.702 * gate_value)) * (up_value + 1.0)
        ).astype(BF16)
        for columns in (slice(0, HALF), slice(HALF, D)):
            arrived[:, columns] = jnp.dot(
                activated[...], down[:, columns], preferred_element_type=F32
            ).astype(BF16)
        for block in range(GROUP // BLOCK):
            landed[pl.ds(first + block * BLOCK, BLOCK)] = pack(mixer_t[...], arrived, block)

        @pl.when(group == OWN // GROUP)
        def _():
            pltpu.make_async_copy(landed.at[OWN], returned.at[OWN], return_sems.at[group]).start()

        each(group, True, lambda slot, target: pltpu.make_async_remote_copy(
            src_ref=landed.at[slot], dst_ref=returned.at[slot], send_sem=result_sem,
            recv_sem=return_sems.at[group], device_id=target, device_id_type=MESH,
        ).start())

    totals[...] = jnp.zeros(totals.shape, F32)

    @pl.loop(0, GROUPS)
    def _(group):
        first = group * GROUP
        span = returned.at[pl.ds(first, GROUP)]
        pltpu.make_async_copy(span, span, return_sems.at[group]).wait()

        for block in range(GROUP // BLOCK):
            unpack(mixer[...], returned[pl.ds(first + block * BLOCK, BLOCK)], arrived, block)

        for start, stop in pieces():
            totals[:, start:stop] += jnp.dot(
                shares[group], arrived[:, start:stop], preferred_element_type=F32
            )

    for start, stop in pieces():
        combined = totals[:TOK, start:stop] * (1.0 / 256.0) + totals[TOK:, start:stop] * (1.0 / 65536.0)
        layer_out = projected[start:stop, :] + jnp.transpose(combined)
        out[start:stop, :] = layer_out.astype(BF16)

    sent = returned.at[pl.ds(1, DEV - 1)]
    pltpu.make_async_copy(sent, sent, send_sem).wait()
    pltpu.make_async_copy(sent, sent, result_sem).wait()
    last_waits()


def shards(attention, out_weight, norm_gain, w_gate, w_up, w_down, routes, gate_fixed):
    near, anywhere = pl.BlockSpec(memory_space=pltpu.VMEM), pl.BlockSpec(memory_space=pl.ANY)
    message = pltpu.VMEM((DEV, ROWS, SLICE), BF16)
    mixer = pltpu.VMEM((BLOCK * ROWS, BLOCK * ROWS), BF16)
    layer_out = pl.pallas_call(
        layer_kernel,
        out_shape=jax.ShapeDtypeStruct((D, TOK), BF16),
        in_specs=[anywhere] * 2 + [near] * 4 + [anywhere] * 3,
        out_specs=near,
        scratch_shapes=[
            pltpu.VMEM((D, TOK), F32),
            pltpu.VMEM((SPAN, 4 * HEAD), BF16),
            pltpu.VMEM((8, COLS, 4 * HEAD), BF16),
            pltpu.VMEM((8, 4, COLS, TOK), BF16),
            pltpu.VMEM((2, 8, COLS, TOK), BF16),
            pltpu.VMEM((8, COLS, TOK), BF16),
            pltpu.SemaphoreType.DMA((5,)),
            pltpu.SemaphoreType.DMA((4, 4)),
            pltpu.SemaphoreType.DMA((4, 8)),
            pltpu.SemaphoreType.DMA((4,)),
            pltpu.SemaphoreType.DMA((2, 8)),
            pltpu.SemaphoreType.DMA((8,)),
            pltpu.SemaphoreType.DMA((6,)),
            pltpu.VMEM((FFW, D), BF16),
            pltpu.VMEM((FFW, D), BF16),
            pltpu.VMEM((FFW, D), BF16),
            message,
            message,
            message,
            pltpu.VMEM((GROWS, WIDE), BF16),
            pltpu.VMEM((GROWS, FFW), BF16),
            pltpu.VMEM((TOK, WIDE), BF16),
            pltpu.VMEM((GROUPS, GROWS, TOK), BF16),
            pltpu.VMEM((GROUPS, 2 * TOK, GROWS), BF16),
            pltpu.VMEM((2 * TOK, D), F32),
            mixer,
            mixer,
            pltpu.SemaphoreType.DMA((3,)),
            pltpu.SemaphoreType.DMA,
            pltpu.SemaphoreType.DMA((GROUPS,)),
            pltpu.SemaphoreType.DMA,
            pltpu.SemaphoreType.DMA((GROUPS,)),
        ],
        compiler_params=pltpu.CompilerParams(
            vmem_limit_bytes=VMEM, collective_id=0, has_side_effects=True
        ),
    )(
        attention[0], jnp.swapaxes(out_weight, 0, 1), norm_gain,
        jnp.swapaxes(routes[0], 0, 1), jnp.swapaxes(gate_fixed[0], 0, 1), row_offsets(),
        jnp.swapaxes(w_gate, 1, 2), jnp.swapaxes(w_up, 1, 2), w_down,
    )
    return jnp.swapaxes(layer_out, 0, 1)[None]


def solution(mesh):
    in_specs = (
        P("exp", None, "ctx"),
        P("ctx", "exp"),
        P(),
        P(("ctx", "exp"), None, None),
        P(("ctx", "exp"), None, None),
        P(("ctx", "exp"), None, None),
        P("exp", "ctx", None),
        P("exp", "ctx", None),
    )
    out_specs = P("exp", "ctx", None)
    return jax.shard_map(shards, mesh=mesh, in_specs=in_specs, out_specs=out_specs, check_vma=False)
```

```python
import jax
import jax.numpy as jnp
import numpy as np
from jax import lax
from jax.experimental import pallas as pl
from jax.experimental.pallas import tpu as pltpu
from jax.sharding import PartitionSpec as P

MESH = pl.DeviceIdType.MESH
BF16, F32, I32 = jnp.bfloat16, jnp.float32, jnp.int32
NT = (((1,), (1,)), ((), ()))

D = 2880
FFW = 1440
TOK = 128
HEAD = 256
COLS = 360
SPAN = 4 * TOK
CAP = 6
DEV = 128
SLICE = 384
PIECES = 8
WIDE = SLICE * PIECES
ROWS = PIECES * CAP
BLOCK = 4
BROWS = BLOCK * CAP
LAYER = 8 // BLOCK
GROUP = 32
GROUPS = DEV // GROUP
GROWS = GROUP * CAP
LAYERS = GROUP // 8


def hops(offset):
    return sum(min(step, 4 - step) for step in offset[:3])


def spread(offset):
    return (offset[0] * 5 + offset[1] * 3 + offset[2] * 7 + offset[3] * 4) % 11


OFFSETS = sorted(
    ((dz, dy, dx, dc) for dz in range(4) for dy in range(4) for dx in range(4) for dc in range(2)),
    key=lambda offset: (hops(offset), spread(offset) * 7 % 11, offset),
)
OWN = OFFSETS.index((0, 0, 0, 0))
VMEM = 62 * 1024 * 1024


def ahead():
    ctx, exp = lax.axis_index("ctx"), lax.axis_index("exp")
    z, y = lax.div(ctx, 4), lax.rem(ctx, 4)
    x, core = lax.div(exp, 2), lax.rem(exp, 2)
    zs = [lax.rem(z + step, 4) for step in range(4)]
    ys = [lax.rem(y + step, 4) for step in range(4)]
    xs = [lax.rem(x + step, 4) for step in range(4)]
    cores = [core, 1 - core]
    return zs, ys, xs, cores


def project(
    place, meanwhile, attention, weight, projected, heads, wide, partial, sums, hop,
    own_sems, head_sems, wide_sems, half_sems, part_sems, hop_sems, send_sems,
):
    zs, ys, xs, cores = place

    def device(dz=0, dy=0, dx=0, dc=0):
        return zs[dz] * 4 + ys[dy], xs[dx] * 2 + cores[dc]

    def lanes(dz, start=0, count=HEAD):
        return pl.ds(dz * HEAD + start, count)

    def remote(source, target, send, receive, **offset):
        pltpu.make_async_remote_copy(
            src_ref=source, dst_ref=target, send_sem=send_sems.at[send], recv_sem=receive,
            device_id=device(**offset), device_id_type=MESH,
        ).start()

    def arrival(target, semaphore):
        pltpu.make_async_copy(target, target, semaphore).wait()

    def tokens(dz, dy):
        return attention.at[pl.ds(pl.multiple_of(zs[dz] * SPAN + ys[dy] * TOK, TOK), TOK)]

    def head_block(dz, dy):
        return heads.at[pl.ds(dy * TOK, TOK), lanes(dz)]

    own = [pltpu.make_async_copy(weight, wide.at[0, :, lanes(0)], own_sems.at[4])]
    own = [
        pltpu.make_async_copy(tokens(0, dy), head_block(0, dy), own_sems.at[dy]) for dy in range(4)
    ] + own
    for copy in own:
        copy.start()
    barrier = pltpu.get_barrier_semaphore()
    friends = (
        [dict(dz=d) for d in (1, 2, 3)] + [dict(dy=d) for d in (1, 3)]
        + [dict(dx=1), dict(dx=3), dict(dc=1)]
    )
    for offset in friends:
        pl.semaphore_signal(barrier, inc=1, device_id=device(**offset), device_id_type=MESH)
    pl.semaphore_wait(barrier, len(friends))

    for dz in (1, 3, 2):
        remote(weight, wide.at[0, :, lanes(dz)], 0, wide_sems.at[dz, 0], dz=dz)

    def across(dz, dx):
        slot = wide.at[2 * dx, :, lanes(dz)]
        remote(slot, wide.at[2 * dx + 1, :, lanes(dz)], 2, wide_sems.at[dz, 2 * dx + 1], dc=1)

    def sideways(dz):
        slot = wide.at[0, :, lanes(dz)]
        if dz:
            arrival(slot, wide_sems.at[dz, 0])
        else:
            own[4].wait()
        for dx in (1, 3):
            remote(slot, wide.at[2 * dx, :, lanes(dz)], 3, wide_sems.at[dz, 2 * dx], dx=dx)
        across(dz, 0)

    def relay(dz):
        for dx, start, semaphore in ((1, 0, wide_sems.at[dz, 4]), (3, 128, half_sems.at[dz])):
            arrival(wide.at[2 * dx, :, lanes(dz)], wide_sems.at[dz, 2 * dx])
            remote(
                wide.at[2 * dx, :, lanes(dz, start, 128)], wide.at[4, :, lanes(dz, start, 128)],
                4, semaphore, dx=dx,
            )
            across(dz, dx)

    def far(dz):
        arrival(wide.at[4, :, lanes(dz, 0, 128)], wide_sems.at[dz, 4])
        arrival(wide.at[4, :, lanes(dz, 128, 128)], half_sems.at[dz])
        across(dz, 2)

    def ready(group):
        if group % 2:
            for dz in range(4):
                arrival(wide.at[group, :, lanes(dz)], wide_sems.at[dz, group])

    def ready_heads(dy):
        own[dy].wait()
        for dz in (1, 3, 2):
            arrival(head_block(dz, dy), head_sems.at[dz, dy])

    def multiply(group, blocks):
        rows = heads[blocks[0] * TOK : (blocks[-1] + 1) * TOK, :]
        product = lax.dot_general(wide[group], rows, NT, preferred_element_type=F32).astype(BF16)
        for place, dy in enumerate(blocks):
            partial[group, dy] = product[:, place * TOK : (place + 1) * TOK]

    def via(group):
        return 3 if group % 2 else 1

    def send_hop(group):
        remote(partial.at[group, 2], hop.at[group], 5, hop_sems.at[group], dy=via(group))

    def send_plain(group):
        dy = 4 - via(group)
        remote(partial.at[group, dy], sums.at[dy // 2, group], 5, part_sems.at[dy // 2, group], dy=dy)

    def send_joined(group):
        dy = via(group)
        arrival(hop.at[group], hop_sems.at[group])
        partial[group, dy] = (partial[group, dy].astype(F32) + hop[group].astype(F32)).astype(BF16)
        remote(partial.at[group, dy], sums.at[dy // 2, group], 5, part_sems.at[dy // 2, group], dy=dy)

    def collect(group):
        total = partial[group, 0].astype(F32)
        for side in range(2):
            arrival(sums.at[side, group], part_sems.at[side, group])
            total = total + sums[side, group].astype(F32)
        total = total.astype(BF16).astype(F32)
        column = xs[(4 - group // 2) % 4] * 2 + cores[group % 2]
        projected[pl.ds(pl.multiple_of(column * COLS, 8), COLS), :] = total
        return jnp.sum(total * total, axis=0, keepdims=True)

    def send_heads(dy):
        for dz in (1, 3, 2):
            remote(tokens(dz, dy), head_block(dz, dy), 1, head_sems.at[dz, dy], dz=dz)

    sideways(0)
    sideways(1)
    sideways(3)
    send_heads(2)
    relay(0)
    sideways(2)
    send_heads(3)
    send_heads(1)
    relay(1)
    meanwhile()
    ready_heads(2)
    send_heads(0)
    multiply(0, (2,))
    send_hop(0)
    relay(3)
    ready(1)
    multiply(1, (2,))
    send_hop(1)
    ready_heads(3)
    multiply(0, (3,))
    send_plain(0)
    relay(2)
    multiply(1, (3,))
    ready_heads(1)
    multiply(1, (1,))
    send_plain(1)
    multiply(0, (1,))
    send_joined(0)
    send_joined(1)
    ready_heads(0)
    multiply(0, (0,))
    multiply(1, (0,))
    previous = None
    for group in (2, 6, 3, 7, 4, 5):
        if group == 3:
            far(0)
            far(1)
        if group == 4:
            far(3)
            far(2)
        ready(group)
        multiply(group, (0, 1, 2, 3))
        send_hop(group)
        send_plain(group)
        if previous is not None:
            send_joined(previous)
        previous = group
    send_joined(previous)
    squares = jnp.zeros((1, TOK), F32)
    for group in (0, 1, 2, 6, 3, 7, 4, 5):
        squares = squares + collect(group)
    sent = enumerate((
        wide.at[0, :, pl.ds(0, 3 * HEAD)],
        heads.at[:, pl.ds(0, 3 * HEAD)],
        wide.at[pl.ds(0, 4)],
        wide.at[pl.ds(0, 2)],
        wide.at[0],
        partial.at[:, pl.ds(0, 3)],
    ))
    return squares, lambda: [arrival(target, send_sems.at[index]) for index, target in sent]


def unpack(mixer, messages, rows, block):
    flat = messages.reshape(BLOCK * ROWS, SLICE)
    sorted_rows = jnp.dot(mixer, flat, preferred_element_type=F32).astype(BF16)
    for piece in range(PIECES):
        rows[block * BROWS : (block + 1) * BROWS, piece * SLICE : (piece + 1) * SLICE] = sorted_rows[
            piece * BROWS : (piece + 1) * BROWS
        ]


def pack(mixer_t, rows, block):
    stacked = jnp.concatenate(
        [
            rows[block * BROWS : (block + 1) * BROWS, piece * SLICE : (piece + 1) * SLICE]
            for piece in range(PIECES)
        ],
        axis=0,
    )
    mixed = jnp.dot(mixer_t, stacked, preferred_element_type=F32).astype(BF16)
    return mixed.reshape(BLOCK, ROWS, SLICE)


def sixth(value):
    whole = (value * 43) >> 8
    return whole, value - 6 * whole


def mixed_places(place):
    piece, position = sixth(place >> 2)
    return (place & 3) * ROWS + piece * CAP + position


def write_mixers(mixer, mixer_t):
    count = BLOCK * ROWS
    source = mixed_places(lax.broadcasted_iota(I32, (count, count), 0))
    place = lax.broadcasted_iota(I32, (count, count), 1)
    mixer[...] = jnp.where(source == place, 1.0, 0.0).astype(BF16)
    source = mixed_places(place)
    place = lax.broadcasted_iota(I32, (count, count), 0)
    mixer_t[...] = jnp.where(source == place, 1.0, 0.0).astype(BF16)


def slot_columns(offsets, zs, ys, xs, cores):
    position = sixth(lax.broadcasted_iota(I32, (1, GROWS), 1) >> 2)[1]
    dz, dy, dx, dc = offsets >> 5, (offsets >> 3) & 3, (offsets >> 1) & 3, offsets & 1
    z, y = (zs[0] + dz) & 3, (ys[0] + dy) & 3
    x, core = (xs[0] + dx) & 3, (cores[0] + dc) & 1
    return (z * 4 + y) * 8 + x * 2 + core, position


def row_offsets():
    row = np.arange(DEV * CAP)
    slot = row // BROWS * BLOCK + row % BLOCK
    numbers = np.array([dz * 32 + dy * 8 + dx * 2 + dc for dz, dy, dx, dc in OFFSETS], np.int32)
    return jnp.asarray(numbers[slot].reshape(GROUPS, 1, GROWS))


HALF = 1408


def pieces():
    return [(start, min(start + SLICE, D)) for start in range(0, D, SLICE)]


def layer_kernel(
    attention, out_weight, gain, routes, gate_fixed, row_offset, w_gate, w_up, w_down,
    out,
    projected, heads, wide, partial, sums, hop,
    own_sems, head_sems, wide_sems, half_sems, part_sems, hop_sems, part_send_sems,
    gate, up, down, send, landed, returned, arrived, activated, normed,
    chooser, shares, totals, mixer, mixer_t,
    weight_sems, send_sem, land_sems, result_sem, return_sems,
):
    loads = [
        pltpu.make_async_copy(source.at[0], target, weight_sems.at[i])
        for i, (source, target) in enumerate(((w_gate, gate), (w_up, up), (w_down, down)))
    ]
    place = ahead()
    zs, ys, xs, cores = place

    def each(group, back, act, layers=range(LAYERS)):
        sign = -1 if back else 1

        def some(first, count):
            for slot in range(first, first + count):
                dz, dy, dx, dc = OFFSETS[slot]
                if slot != OWN:
                    target = (
                        zs[sign * dz % 4] * 4 + ys[sign * dy % 4],
                        xs[sign * dx % 4] * 2 + cores[dc],
                    )
                    act(slot, target)

        for here in range(GROUPS):
            for layer in layers:
                pl.when(group == here)(lambda: some(here * GROUP + layer * 8, 8))

    def prepare():
        write_mixers(mixer, mixer_t)
        earlier = lax.broadcasted_iota(I32, (TOK, TOK), 1) < lax.broadcasted_iota(I32, (TOK, TOK), 0)
        earlier = jnp.where(earlier, 1.0, 0.0).astype(BF16)

        named_experts = jnp.transpose(routes[...])
        named_shares = jnp.transpose(gate_fixed[...])

        @pl.loop(0, GROUPS)
        def _(group):
            expert, position = slot_columns(row_offset[group], zs, ys, xs, cores)
            fixed = jnp.zeros((TOK, GROWS), I32)
            for k in range(4):
                named = named_experts[:, k : k + 1] == expert
                fixed = fixed + jnp.where(named, named_shares[:, k : k + 1], 0)
            chosen = jnp.where(fixed > 0, 1.0, 0.0)
            rank = jnp.dot(earlier, chosen.astype(BF16), preferred_element_type=F32)
            mask = (fixed > 0) & (rank == position.astype(F32))
            fixed = jnp.where(mask, fixed, 0)
            shares[group, :TOK] = (fixed >> 8).astype(F32).astype(BF16)
            shares[group, TOK:] = (fixed & 255).astype(F32).astype(BF16)
            chooser[group] = jnp.transpose(jnp.where(mask, 1.0, 0.0)).astype(BF16)

    squares, last_waits = project(
        place, prepare, attention, out_weight, projected, heads, wide, partial, sums, hop,
        own_sems, head_sems, wide_sems, half_sems, part_sems, hop_sems, part_send_sems,
    )
    for load in loads:
        load.start()
    scale = lax.rsqrt(squares / D + 1e-05)
    normed[:, D:] = jnp.zeros((TOK, WIDE - D), BF16)
    for start, stop in pieces():
        scaled = jnp.transpose(projected[start:stop, :] * scale)
        normed[:, start:stop] = (scaled * gain[start:stop].reshape(1, stop - start)).astype(BF16)

    @pl.loop(0, GROUPS)
    def _(group):
        first = group * GROUP
        for piece in range(PIECES):
            columns = pl.ds(piece * SLICE, SLICE)
            arrived[:, columns] = jnp.dot(
                chooser[group], normed[:, columns], preferred_element_type=F32
            ).astype(BF16)

        for layer in range(4):
            for block in range(layer * LAYER, layer * LAYER + LAYER):
                send[pl.ds(first + block * BLOCK, BLOCK)] = pack(mixer_t[...], arrived, block)
            if layer == OWN % GROUP // 8:
                @pl.when(group == OWN // GROUP)
                def _():
                    pltpu.make_async_copy(send.at[OWN], landed.at[OWN], land_sems.at[group]).start()

            each(group, False, lambda slot, target: pltpu.make_async_remote_copy(
                src_ref=send.at[slot], dst_ref=landed.at[slot], send_sem=send_sem,
                recv_sem=land_sems.at[group], device_id=target, device_id_type=MESH,
            ).start(), [layer])

    for load in loads:
        load.wait()

    @pl.loop(0, GROUPS)
    def _(group):
        first = group * GROUP
        span = landed.at[pl.ds(first, GROUP)]
        pltpu.make_async_copy(span, span, land_sems.at[group]).wait()

        for block in range(GROUP // BLOCK):
            unpack(mixer[...], landed[pl.ds(first + block * BLOCK, BLOCK)], arrived, block)

        gate_value = lax.dot_general(arrived[:, :D], gate[...], NT, preferred_element_type=F32)
        up_value = lax.dot_general(arrived[:, :D], up[...], NT, preferred_element_type=F32)
        activated[...] = (
            gate_value / (1.0 + jnp.exp(-1.702 * gate_value)) * (up_value + 1.0)
        ).astype(BF16)
        for columns in (slice(0, HALF), slice(HALF, D)):
            arrived[:, columns] = jnp.dot(
                activated[...], down[:, columns], preferred_element_type=F32
            ).astype(BF16)
        for block in range(GROUP // BLOCK):
            landed[pl.ds(first + block * BLOCK, BLOCK)] = pack(mixer_t[...], arrived, block)

        @pl.when(group == OWN // GROUP)
        def _():
            pltpu.make_async_copy(landed.at[OWN], returned.at[OWN], return_sems.at[group]).start()

        each(group, True, lambda slot, target: pltpu.make_async_remote_copy(
            src_ref=landed.at[slot], dst_ref=returned.at[slot], send_sem=result_sem,
            recv_sem=return_sems.at[group], device_id=target, device_id_type=MESH,
        ).start())

    totals[...] = jnp.zeros(totals.shape, F32)

    @pl.loop(0, GROUPS)
    def _(group):
        first = group * GROUP
        span = returned.at[pl.ds(first, GROUP)]
        pltpu.make_async_copy(span, span, return_sems.at[group]).wait()

        for block in range(GROUP // BLOCK):
            unpack(mixer[...], returned[pl.ds(first + block * BLOCK, BLOCK)], arrived, block)

        for start, stop in pieces():
            totals[:, start:stop] += jnp.dot(
                shares[group], arrived[:, start:stop], preferred_element_type=F32
            )

    for start, stop in pieces():
        combined = totals[:TOK, start:stop] * (1.0 / 256.0) + totals[TOK:, start:stop] * (1.0 / 65536.0)
        layer_out = projected[start:stop, :] + jnp.transpose(combined)
        out[start:stop, :] = layer_out.astype(BF16)

    sent = returned.at[pl.ds(1, DEV - 1)]
    pltpu.make_async_copy(sent, sent, send_sem).wait()
    pltpu.make_async_copy(sent, sent, result_sem).wait()
    last_waits()


def shards(attention, out_weight, norm_gain, w_gate, w_up, w_down, routes, gate_fixed):
    near, anywhere = pl.BlockSpec(memory_space=pltpu.VMEM), pl.BlockSpec(memory_space=pl.ANY)
    message = pltpu.VMEM((DEV, ROWS, SLICE), BF16)
    mixer = pltpu.VMEM((BLOCK * ROWS, BLOCK * ROWS), BF16)
    layer_out = pl.pallas_call(
        layer_kernel,
        out_shape=jax.ShapeDtypeStruct((D, TOK), BF16),
        in_specs=[anywhere] * 2 + [near] * 4 + [anywhere] * 3,
        out_specs=near,
        scratch_shapes=[
            pltpu.VMEM((D, TOK), F32),
            pltpu.VMEM((SPAN, 4 * HEAD), BF16),
            pltpu.VMEM((8, COLS, 4 * HEAD), BF16),
            pltpu.VMEM((8, 4, COLS, TOK), BF16),
            pltpu.VMEM((2, 8, COLS, TOK), BF16),
            pltpu.VMEM((8, COLS, TOK), BF16),
            pltpu.SemaphoreType.DMA((5,)),
            pltpu.SemaphoreType.DMA((4, 4)),
            pltpu.SemaphoreType.DMA((4, 8)),
            pltpu.SemaphoreType.DMA((4,)),
            pltpu.SemaphoreType.DMA((2, 8)),
            pltpu.SemaphoreType.DMA((8,)),
            pltpu.SemaphoreType.DMA((6,)),
            pltpu.VMEM((FFW, D), BF16),
            pltpu.VMEM((FFW, D), BF16),
            pltpu.VMEM((FFW, D), BF16),
            message,
            message,
            message,
            pltpu.VMEM((GROWS, WIDE), BF16),
            pltpu.VMEM((GROWS, FFW), BF16),
            pltpu.VMEM((TOK, WIDE), BF16),
            pltpu.VMEM((GROUPS, GROWS, TOK), BF16),
            pltpu.VMEM((GROUPS, 2 * TOK, GROWS), BF16),
            pltpu.VMEM((2 * TOK, D), F32),
            mixer,
            mixer,
            pltpu.SemaphoreType.DMA((3,)),
            pltpu.SemaphoreType.DMA,
            pltpu.SemaphoreType.DMA((GROUPS,)),
            pltpu.SemaphoreType.DMA,
            pltpu.SemaphoreType.DMA((GROUPS,)),
        ],
        compiler_params=pltpu.CompilerParams(
            vmem_limit_bytes=VMEM, collective_id=0, has_side_effects=True
        ),
    )(
        attention[0], jnp.swapaxes(out_weight, 0, 1), norm_gain,
        jnp.swapaxes(routes[0], 0, 1), jnp.swapaxes(gate_fixed[0], 0, 1), row_offsets(),
        jnp.swapaxes(w_gate, 1, 2), jnp.swapaxes(w_up, 1, 2), w_down,
    )
    return jnp.swapaxes(layer_out, 0, 1)[None]


def solution(mesh):
    in_specs = (
        P("exp", None, "ctx"),
        P("ctx", "exp"),
        P(),
        P(("ctx", "exp"), None, None),
        P(("ctx", "exp"), None, None),
        P(("ctx", "exp"), None, None),
        P("exp", "ctx", None),
        P("exp", "ctx", None),
    )
    out_specs = P("exp", "ctx", None)
    return jax.shard_map(shards, mesh=mesh, in_specs=in_specs, out_specs=out_specs, check_vma=False)
```
